1024 devices in a mesh: cells: 128 (over z, x, core), grp: 8 (over y).
Axes of the slice: x: 8, y: 8, z: 8, core: 2. Of those that a mesh axis runs over, the one named last changes fastest.
Arguments:
- multipoles: bfloat16 [165, 131072], P(None, ('cells', 'grp')), may hold values from -6 to 6
- operators: bfloat16 [165, 165, 128], replicated, may hold values from -0.0625 to 0.0625
- local_pairs: int32 [1024, 16, 2, 256], P(('cells', 'grp')), may hold values from 0 to 127, as said below
- group_pairs: int32 [1024, 8, 2, 256], P(('cells', 'grp')), may hold values from 0 to 127, as said below
- far_pairs: int32 [1024, 8, 2, 256], P(('cells', 'grp')), may hold values from 0 to 127, as said below
- batch_class: int32 [1024, 32], P(('cells', 'grp')), may hold values from 0 to 127
- batch_count: int32 [1024, 32], P(('cells', 'grp')), may hold values from 64 to 256, as said below
- group_send: int32 [128, 8, 8, 8], P('cells'), may hold values from 0 to 127
- far_send: int32 [1024, 128, 1], P(('cells', 'grp')), may hold values from 0 to 127
Outputs:
- local_expansions: float32 [165, 131072], P(None, ('cells', 'grp'))
The draws below stay inside these ranges and needn't reach their ends.
Inputs may be any that keep to these rules, and one draw needn't show every extreme that they name: `local_pairs`: the two cells of a pair differ. `group_pairs`: entry 0 is a cell of the block, entry 1 a received slot below 64. `far_pairs`: entry 0 is a cell of the block, entry 1 a received slot below 128. `batch_count`: every block has a full batch.
All inputs are finite; a program needn't handle non-finite values.
Results may differ from the reference program's by a relative error of at most 0.0003.
Values may be sent and summed in bfloat16 or wider, within the bound.
No kernel may reach another device: no remote copies, remote signals or barrier semaphores. Data moves between devices by JAX's collectives and lax.ppermute only.
A program may use at most 64 MiB of HBM per device.

```python
import jax
import jax.numpy as jnp
from jax import lax

ORDER = 8
COEFFS = 165
CLASSES = 128
BATCH = 256
CELL_DEV = 128
LOCAL_B = 16
GROUP_B = 8
FAR_B = 8
SLOT_GROUP = 8
SLOT_FAR = 1
BATCHES = 32
BLOCKS = 1024
CELLS = 131072
N_CELLS = 128
N_GRP = 8


def remote_pairs(key, batches, received):
    first, second = jax.random.split(key)
    targets = jax.random.randint(first, (BLOCKS, batches, BATCH), 0, CELL_DEV, dtype=jnp.int32)
    arrivals = jax.random.randint(second, (BLOCKS, batches, BATCH), 0, received, dtype=jnp.int32)
    targets = targets.at[0, 0, 0].set(CELL_DEV - 1).at[0, 0, 1].set(0)
    arrivals = arrivals.at[0, 0, 0].set(received - 1).at[0, 0, 1].set(0)
    return jnp.stack([targets, arrivals], axis=2)


def draw_local_pairs(key, part):
    key = jax.random.fold_in(key, 3)
    first, second = jax.random.split(key)
    targets = jax.random.randint(first, (BLOCKS, LOCAL_B, BATCH), 0, CELL_DEV, dtype=jnp.int32)
    offsets = jax.random.randint(second, (BLOCKS, LOCAL_B, BATCH), 1, CELL_DEV, dtype=jnp.int32)
    targets = targets.at[0, 0, 0].set(CELL_DEV - 1).at[0, 0, 1].set(0)
    sources = (targets + offsets) % CELL_DEV
    return jnp.stack([targets, sources], axis=2).astype(jnp.int32)


def draw_group_pairs(key, part):
    key = jax.random.fold_in(key, 5)
    return remote_pairs(key, GROUP_B, N_GRP * SLOT_GROUP)


def draw_far_pairs(key, part):
    key = jax.random.fold_in(key, 9)
    return remote_pairs(key, FAR_B, N_CELLS * SLOT_FAR)


def draw_batch_count(key, part):
    key = jax.random.fold_in(key, 7)
    first, second = jax.random.split(key)
    counts = jax.random.randint(first, (BLOCKS, BATCHES), BATCH // 4, BATCH + 1, dtype=jnp.int32)
    full_at = jax.random.randint(second, (BLOCKS, 1), 0, BATCHES, dtype=jnp.int32)
    filled = jnp.arange(BATCHES, dtype=jnp.int32)[None, :] == full_at
    return jnp.where(filled, BATCH, counts).astype(jnp.int32)


def touch_ends(result, own_key, smallest, top_value):
    spot = [jax.random.randint(jax.random.fold_in(own_key, axis), (), 0, length) for axis, length in enumerate(result.shape)]
    longest = result.shape.index(max(result.shape))
    next_to = spot[:longest] + [(spot[longest] + 1) % result.shape[longest]] + spot[longest + 1:]
    return result.at[tuple(spot)].set(smallest).at[tuple(next_to)].set(top_value)


def block_levels(own_key, dims, cuts, smallest, top_value):
    loudness = 1.0
    for axis_at, shards_of in cuts:
        draws = jax.random.uniform(jax.random.fold_in(jax.random.fold_in(own_key, 6), axis_at), (shards_of,), jnp.float32, smallest / len(cuts), top_value / len(cuts))
        loudness = loudness * jnp.repeat(jnp.exp(draws), dims[axis_at] // shards_of).reshape((-1,) + (1,) * (len(dims) - 1 - axis_at))
    return loudness


def noise(key, shape, spread, most, cuts=(), held_as=jnp.bfloat16):
    result = jax.random.normal(key, shape, jnp.float32) * spread
    if len(cuts) > 0:
        result = block_levels(key, shape, cuts, -0.22, 0.18) * result
    return jnp.clip(result, min=-most, max=most).astype(held_as)


def setup_inputs(seed: int = 0) -> dict:
    splits = jax.random.split(jax.random.key(seed), 10)
    multipoles = noise(splits[0], (COEFFS, CELLS), 1.0, 6.0, ((1, 1024),))
    operators = noise(splits[1], (COEFFS, COEFFS, CLASSES), (COEFFS * 48) ** -0.5, 0.0625)
    local_pairs = draw_local_pairs(jax.random.fold_in(splits[9], 71), 0)
    group_pairs = draw_group_pairs(jax.random.fold_in(splits[9], 71), 0)
    far_pairs = draw_far_pairs(jax.random.fold_in(splits[9], 71), 0)
    batch_class = touch_ends(jax.random.randint(splits[5], (BLOCKS, BATCHES), 0, CLASSES), jax.random.fold_in(splits[5], 1), 0, CLASSES - 1).astype(jnp.int32)
    batch_count = draw_batch_count(jax.random.fold_in(splits[9], 71), 0)
    group_send = touch_ends(jax.random.randint(splits[7], (N_CELLS, N_GRP, N_GRP, SLOT_GROUP), 0, CELL_DEV), jax.random.fold_in(splits[7], 1), 0, CELL_DEV - 1).astype(jnp.int32)
    far_send = touch_ends(jax.random.randint(splits[8], (BLOCKS, N_CELLS, SLOT_FAR), 0, CELL_DEV), jax.random.fold_in(splits[8], 1), 0, CELL_DEV - 1).astype(jnp.int32)
    return {"multipoles": multipoles, "operators": operators, "local_pairs": local_pairs, "group_pairs": group_pairs, "far_pairs": far_pairs, "batch_class": batch_class, "batch_count": batch_count, "group_send": group_send, "far_send": far_send}


def degree_signs():
    pieces = [jnp.full(((degree + 1) * (degree + 2) // 2,), (-1.0) ** degree, jnp.float32) for degree in range(ORDER + 1)]
    return jnp.concatenate(pieces)


def reference(multipoles, operators, local_pairs, group_pairs, far_pairs, batch_class, batch_count, group_send, far_send):
    parity = degree_signs()
    positions = jnp.arange(BATCH, dtype=jnp.int32)

    def one_block(block_id, totals):
        block_id = jnp.asarray(block_id).astype(jnp.int32)
        cell_pos = block_id // N_GRP
        group_pos = block_id % N_GRP
        base_cell = block_id * CELL_DEV
        near_list = local_pairs[block_id]
        near_target = base_cell + near_list[:, 0]
        near_source = base_cell + near_list[:, 1]
        group_list = group_pairs[block_id]
        group_target = base_cell + group_list[:, 0]
        group_peer = group_list[:, 1] // SLOT_GROUP
        group_slot = group_list[:, 1] % SLOT_GROUP
        group_cell = group_send[cell_pos, group_peer, group_pos, group_slot]
        group_source = (cell_pos * N_GRP + group_peer) * CELL_DEV + group_cell
        far_list = far_pairs[block_id]
        far_target = base_cell + far_list[:, 0]
        sender = (far_list[:, 1] // SLOT_FAR) * N_GRP + group_pos
        far_cell = far_send[sender, cell_pos, far_list[:, 1] % SLOT_FAR]
        far_source = sender * CELL_DEV + far_cell
        targets = jnp.concatenate([near_target, group_target, far_target], axis=0).astype(jnp.int32)
        sources = jnp.concatenate([near_source, group_source, far_source], axis=0).astype(jnp.int32)
        usable = (positions[None, :] < batch_count[block_id][:, None]).astype(jnp.float32)
        picked = jnp.take(operators, batch_class[block_id], axis=2).astype(jnp.float32)
        target_cols = jnp.take(multipoles, targets, axis=1).astype(jnp.float32) * usable[None]
        source_cols = jnp.take(multipoles, sources, axis=1).astype(jnp.float32) * usable[None]
        to_target = jnp.einsum("knb,nbs->kbs", picked, source_cols, precision=lax.Precision.HIGHEST)
        to_source = parity[:, None, None] * jnp.einsum("knb,nbs->kbs", picked, parity[:, None, None] * target_cols, precision=lax.Precision.HIGHEST)
        return totals.at[:, targets].add(to_target).at[:, sources].add(to_source)

    start = jnp.zeros((COEFFS, CELLS), jnp.float32)
    return lax.fori_loop(0, N_CELLS * N_GRP, one_block, start)
```

```python
import functools

import jax
import jax.numpy as jnp
import numpy as np
from jax import lax
from jax.experimental import pallas as pl
from jax.experimental.pallas import tpu as pltpu
from jax.sharding import PartitionSpec as P

ORDER = 8
LANES = 128
WIDE = 256
PAD_ROWS = 176
STEP_ROWS = 15
BF = jnp.bfloat16
F32 = jnp.float32
VMEM_LIMIT = 56 * 1024 * 1024


def degree_signs():
    return np.concatenate(
        [np.full(((d + 1) * (d + 2) // 2,), (-1.0) ** d, np.float32) for d in range(ORDER + 1)]
    )


def lane_signs():
    signs = np.zeros((1, WIDE), np.float32)
    signs[0, : degree_signs().size] = degree_signs()
    return signs


def dot_nt(a, b):
    return lax.dot_general(a, b, (((1,), (1,)), ((), ())), preferred_element_type=F32)


def dot_nn(a, b):
    return lax.dot_general(a, b, (((1,), (0,)), ((), ())), preferred_element_type=F32)


def split(x):
    high = x.astype(BF)
    low = (x - high.astype(F32)).astype(BF)
    return high, low


def one_hot(ids, size):
    rows = lax.broadcasted_iota(jnp.int32, (size, ids.shape[1]), 0)
    return jnp.where(rows == ids, 1.0, 0.0).astype(BF)


def pair_hots(pairs_ref, batch, count, first, second):
    targets = pairs_ref[0, batch, 0:1, :]
    sources = pairs_ref[0, batch, 1:2, :]
    spots = lax.broadcasted_iota(jnp.int32, targets.shape, 1)
    targets = jnp.where(spots < count, targets, -1)
    return one_hot(targets, first), one_hot(sources, second)


def padded_rows(own):
    own = own.astype(F32)
    return jnp.concatenate([own, jnp.zeros((WIDE - own.shape[0], own.shape[1]), F32)], axis=0)


def scalar_row(read, count):
    lanes = lax.broadcasted_iota(jnp.int32, (1, LANES), 1)
    row = jnp.full((1, LANES), -1, jnp.int32)
    for i in range(count):
        row = jnp.where(lanes == i, read(i), row)
    return row


def prepare_kernel(
    batch_class, batch_count, me, group_send, own_ref, ops_ref, group_ref, far_ref, far_send_ref,
    signs_ref, far_out, group_out, near_ops, rest_ops, hot_class, low_table, high_table,
):
    step = pl.program_id(0)
    batches = batch_class.shape[1]
    coeffs = own_ref.shape[0]
    cells = own_ref.shape[1]
    near = near_ops.shape[0]
    group_batches = group_ref.shape[1]
    far_batches = far_ref.shape[1]
    group_slots = group_out.shape[0]
    far_slots = far_out.shape[0] // 4

    @pl.when(step == 0)
    def _():
        rows = lax.broadcasted_iota(jnp.int32, (batches, LANES), 0)
        lanes = lax.broadcasted_iota(jnp.int32, (batches, LANES), 1)
        wanted = jnp.zeros((batches, LANES), jnp.int32)
        for i in range(batches):
            wanted = jnp.where(rows == i, batch_class[0, i], wanted)
        hot_class[...] = jnp.where(lanes == wanted, 1.0, 0.0).astype(BF)
        high_table[...] = jnp.zeros(high_table.shape, F32)
        low_table[coeffs * batches :, :] = jnp.zeros(((PAD_ROWS - coeffs) * batches, LANES), F32)

    hot = hot_class[...]
    for i in range(STEP_ROWS):
        picked = dot_nt(hot, ops_ref[i])
        start = pl.multiple_of((step * STEP_ROWS + i) * batches, batches)
        low_table[pl.ds(start, batches), :] = picked[:, :LANES]
        high_table[pl.ds(start, batches), : coeffs - LANES] = picked[:, LANES:]

    @pl.when(step == pl.num_programs(0) - 1)
    def _():
        def matrix(i):
            low = low_table[pl.ds(i, PAD_ROWS, stride=batches), :]
            high = high_table[pl.ds(i, PAD_ROWS, stride=batches), :]
            return jnp.concatenate([low, high], axis=1).astype(BF)

        signs = signs_ref[...]
        own = padded_rows(own_ref[...])
        own_half = own.astype(BF)
        sign_column = jnp.transpose(jnp.broadcast_to(signs, (LANES, WIDE)))
        flipped = (own * sign_column[:, :cells]).astype(BF)

        def back_terms(pairs_ref, count_batches, first_batch, slots):
            counts = []
            for b in range(count_batches):
                hot_t, hot_u = pair_hots(
                    pairs_ref, b, batch_count[0, first_batch + b], cells, slots
                )
                counts.append(dot_nt(hot_u, hot_t).astype(BF))
            summed = dot_nt(jnp.concatenate(counts, axis=0), flipped)
            total = jnp.zeros((slots, PAD_ROWS), F32)
            for b in range(count_batches):
                high, low = split(summed[b * slots : (b + 1) * slots])
                both = dot_nt(jnp.concatenate([high, low], axis=0), matrix(first_batch + b))
                total = total + both[:slots] + both[slots:]
            return total * signs[:, :PAD_ROWS]

        far_back = back_terms(far_ref, far_batches, near + group_batches, far_slots)
        far_hot = one_hot(far_send_ref[...], cells)
        far_own = jnp.transpose(dot_nn(own_half, far_hot))
        far_out[pl.ds(0, far_slots, stride=4), :] = far_back[:, :LANES]
        far_out[pl.ds(1, far_slots, stride=4), :] = jnp.concatenate(
            [far_back[:, LANES:], jnp.zeros((far_slots, WIDE - PAD_ROWS), F32)], axis=1
        )
        far_out[pl.ds(2, far_slots, stride=4), :] = far_own[:, :LANES]
        far_out[pl.ds(3, far_slots, stride=4), :] = far_own[:, LANES:]

        group_back = back_terms(group_ref, group_batches, near, group_slots)
        row = scalar_row(lambda i: group_send[0, me[0], i // 8, i % 8], group_slots)
        group_hot = one_hot(row, cells)
        group_own = jnp.transpose(dot_nn(own_half, group_hot))[:group_slots]
        group_out[:, :LANES] = group_back[:, :LANES]
        group_out[:, LANES:WIDE] = jnp.concatenate(
            [group_back[:, LANES:], jnp.zeros((group_slots, WIDE - PAD_ROWS), F32)], axis=1
        )
        group_out[:, WIDE:] = group_own
        for i in range(near):
            near_ops[i] = matrix(i)
        for i in range(batches - near):
            rest_ops[i] = matrix(near + i)


def near_kernel(batch_count, own_ref, near_ref, ops_ref, signs_ref, out_ref):
    cells = own_ref.shape[1]
    near = ops_ref.shape[0]
    signs = signs_ref[...]
    own = padded_rows(own_ref[...])
    own_half = own.astype(BF)
    sign_column = jnp.transpose(jnp.broadcast_to(signs, (LANES, WIDE)))
    flipped = (own * sign_column[:, :cells]).astype(BF)
    forward, backward = [], []
    for b in range(near):
        hot_t, hot_u = pair_hots(near_ref, b, batch_count[0, b], cells, cells)
        forward.append(dot_nt(hot_t, hot_u).astype(BF))
        backward.append(dot_nt(hot_u, hot_t).astype(BF))
    ahead = dot_nt(jnp.concatenate(forward, axis=0), own_half)
    behind = dot_nt(jnp.concatenate(backward, axis=0), flipped)
    total = jnp.zeros((cells, PAD_ROWS), F32)
    mirrored = jnp.zeros((cells, PAD_ROWS), F32)
    for b in range(near):
        part = slice(b * cells, (b + 1) * cells)
        both = dot_nt(
            jnp.concatenate([*split(ahead[part]), *split(behind[part])], axis=0), ops_ref[b]
        )
        total = total + both[:cells] + both[cells : 2 * cells]
        mirrored = mirrored + both[2 * cells : 3 * cells] + both[3 * cells :]
    out_ref[...] = total + mirrored * signs[:, :PAD_ROWS]


def finish_kernel(
    batch_count, me, group_send, near_sum, ops_ref, group_ref, far_ref, far_send_ref, far_in,
    group_in, out_ref,
):
    cells = out_ref.shape[1]
    coeffs = out_ref.shape[0]
    group_batches = group_ref.shape[1]
    far_batches = far_ref.shape[1]
    near = batch_count.shape[1] - group_batches - far_batches
    far_slots = far_in.shape[0] // 4
    group_slots = group_in.shape[0]
    total = near_sum[...]

    def forward_terms(pairs_ref, count_batches, first_batch, slots, arrived, total):
        counts = []
        for b in range(count_batches):
            hot_t, hot_u = pair_hots(pairs_ref, b, batch_count[0, near + first_batch + b], cells, slots)
            counts.append(dot_nt(hot_t, hot_u).astype(BF))
        summed = dot_nn(jnp.concatenate(counts, axis=0), arrived)
        for b in range(count_batches):
            high, low = split(summed[b * cells : (b + 1) * cells])
            both = dot_nt(jnp.concatenate([high, low], axis=0), ops_ref[first_batch + b])
            total = total + both[:cells] + both[cells:]
        return total

    def piece(i):
        return far_in[pl.ds(i, far_slots, stride=4), :]

    far_arrived = jnp.concatenate([piece(2), piece(3)], axis=1).astype(BF)
    total = forward_terms(far_ref, far_batches, group_batches, far_slots, far_arrived, total)
    group_arrived = group_in[:, WIDE:].astype(BF)
    total = forward_terms(group_ref, group_batches, 0, group_slots, group_arrived, total)

    far_hot = one_hot(far_send_ref[...], cells)
    home_high, home_low = split(jnp.concatenate([piece(0), piece(1)], axis=1))
    row = scalar_row(lambda i: group_send[0, me[0], i // 8, i % 8], group_slots)
    group_hot = one_hot(row, cells)[:, :group_slots]
    back_high, back_low = split(group_in[:, :WIDE])
    home = dot_nn(far_hot, home_high) + dot_nn(far_hot, home_low)
    home = home + dot_nn(group_hot, back_high) + dot_nn(group_hot, back_low)
    total = total + home[:, :PAD_ROWS]
    total = jnp.concatenate([total, jnp.zeros((cells, WIDE - PAD_ROWS), F32)], axis=1)
    out_ref[...] = jnp.transpose(total)[:coeffs]


def body(
    multipoles, operators, local_pairs, group_pairs, far_pairs, batch_class, batch_count,
    group_send, far_send,
):
    coeffs, cells = multipoles.shape
    batches = batch_class.shape[1]
    near = local_pairs.shape[1]
    group_size = lax.axis_size("grp")
    ranges = lax.axis_size("cells")
    far_slots = far_send.shape[1] * far_send.shape[2]
    far_send = far_send.reshape(1, far_slots)
    group_slots = group_size * group_send.shape[3]
    me = lax.axis_index("grp").reshape(1)
    signs = jnp.asarray(lane_signs())
    smem = pl.BlockSpec(memory_space=pltpu.SMEM)
    vmem = pl.BlockSpec(memory_space=pltpu.VMEM)
    params = pltpu.CompilerParams(vmem_limit_bytes=VMEM_LIMIT)

    def whole(a):
        zeros = (0,) * a.ndim
        return pl.BlockSpec(a.shape, lambda i: zeros)

    def out_block(shape):
        zeros = (0,) * len(shape)
        return pl.BlockSpec(shape, lambda i: zeros)

    shapes = [
        jax.ShapeDtypeStruct((far_slots * 4, LANES), F32),
        jax.ShapeDtypeStruct((group_slots, 2 * WIDE), F32),
    ]
    far_rows, group_rows, ops_near, ops_rest = pl.pallas_call(
        prepare_kernel,
        grid=(coeffs // STEP_ROWS,),
        in_specs=[smem] * 4
        + [
            whole(multipoles),
            pl.BlockSpec((STEP_ROWS,) + operators.shape[1:], lambda i: (i, 0, 0)),
            whole(group_pairs),
            whole(far_pairs),
            whole(far_send),
            whole(signs),
        ],
        out_shape=shapes
        + [
            jax.ShapeDtypeStruct((near, PAD_ROWS, WIDE), BF),
            jax.ShapeDtypeStruct((batches - near, PAD_ROWS, WIDE), BF),
        ],
        out_specs=[
            out_block(shapes[0].shape),
            out_block(shapes[1].shape),
            out_block((near, PAD_ROWS, WIDE)),
            out_block((batches - near, PAD_ROWS, WIDE)),
        ],
        scratch_shapes=[
            pltpu.VMEM((batches, LANES), BF),
            pltpu.VMEM((PAD_ROWS * batches, LANES), F32),
            pltpu.VMEM((PAD_ROWS * batches, LANES), F32),
        ],
        compiler_params=params,
        name="prepare",
    )(
        batch_class, batch_count, me, group_send, multipoles, operators, group_pairs, far_pairs,
        far_send, signs,
    )
    far_got = lax.all_to_all(
        far_rows.reshape(ranges, -1, LANES), "cells", split_axis=0, concat_axis=0, tiled=True
    ).reshape(far_rows.shape)
    group_got = lax.all_to_all(
        group_rows.reshape(group_size, -1, 2 * WIDE), "grp", split_axis=0, concat_axis=0, tiled=True
    ).reshape(group_rows.shape)
    near_sum = pl.pallas_call(
        near_kernel,
        in_specs=[smem] + [vmem] * 4,
        out_specs=vmem,
        out_shape=jax.ShapeDtypeStruct((cells, PAD_ROWS), F32),
        compiler_params=params,
        cost_estimate=pl.CostEstimate(
            flops=20_000_000_000, bytes_accessed=40_000_000, transcendentals=0
        ),
        name="near",
    )(batch_count, multipoles, local_pairs, ops_near, signs)
    return pl.pallas_call(
        finish_kernel,
        in_specs=[smem] * 3 + [vmem] * 7,
        out_specs=vmem,
        out_shape=jax.ShapeDtypeStruct((coeffs, cells), F32),
        compiler_params=params,
        name="finish",
    )(
        batch_count, me, group_send, near_sum, ops_rest, group_pairs, far_pairs, far_send, far_got,
        group_got,
    )


def solution(mesh):
    placed = (
        P(None, ("cells", "grp")),
        P(),
        P(("cells", "grp"), None, None, None),
        P(("cells", "grp"), None, None, None),
        P(("cells", "grp"), None, None, None),
        P(("cells", "grp"), None),
        P(("cells", "grp"), None),
        P("cells", None, None, None),
        P(("cells", "grp"), None, None),
    )
    return jax.shard_map(
        body, mesh=mesh, in_specs=placed, out_specs=P(None, ("cells", "grp")), check_vma=False
    )
```

```python
import jax
import jax.numpy as jnp
import numpy as np
from jax import lax
from jax.experimental import pallas as pl
from jax.experimental.pallas import tpu as pltpu
from jax.sharding import PartitionSpec as P

ORDER = 8
LANES = 128
WIDE = 256
PAD_ROWS = 176
PITCH = 40
CHUNK = 16
SHIFT = 40
BF = jnp.bfloat16
F32 = jnp.float32


def degree_signs():
    return np.concatenate(
        [np.full(((d + 1) * (d + 2) // 2,), (-1.0) ** d, np.float32) for d in range(ORDER + 1)]
    )


def lane_signs():
    signs = np.zeros((1, WIDE), np.float32)
    signs[0, : degree_signs().size] = degree_signs()
    return signs


def dot_nt(a, b):
    return lax.dot_general(a, b, (((1,), (1,)), ((), ())), preferred_element_type=F32)


def dot_nn(a, b):
    return lax.dot_general(a, b, (((1,), (0,)), ((), ())), preferred_element_type=F32)


def split(x):
    high = x.astype(BF)
    low = (x - high.astype(F32)).astype(BF)
    return high, low


def one_hot(ids, size):
    rows = lax.broadcasted_iota(jnp.int32, (size, ids.shape[1]), 0)
    return jnp.where(rows == ids, 1.0, 0.0).astype(BF)


def pair_hots(pairs_ref, batch, count, first, second):
    targets = pairs_ref[0, batch, 0:1, :]
    sources = pairs_ref[0, batch, 1:2, :]
    spots = lax.broadcasted_iota(jnp.int32, targets.shape, 1)
    targets = jnp.where(spots < count, targets, -1)
    return one_hot(targets, first), one_hot(sources, second)


def padded_rows(own):
    own = own.astype(F32)
    return jnp.concatenate([own, jnp.zeros((WIDE - own.shape[0], own.shape[1]), F32)], axis=0)


def scalar_row(read, count):
    lanes = lax.broadcasted_iota(jnp.int32, (1, LANES), 1)
    row = jnp.full((1, LANES), -1, jnp.int32)
    for i in range(count):
        row = jnp.where(lanes == i, read(i), row)
    return row


def pack_tiles(high, low, own):
    tail = high[:, LANES:] + pltpu.roll(low[:, LANES:], SHIFT, 1)
    tail = tail + pltpu.roll(own[:, LANES:], 2 * SHIFT, 1)
    return [high[:, :LANES], low[:, :LANES], own[:, :LANES], tail]


def unpack_tiles(tiles, coeffs):
    tail = tiles[3]
    lanes = lax.broadcasted_iota(jnp.int32, tail.shape, 1)
    parts = []
    for i in range(3):
        moved = tail if i == 0 else pltpu.roll(tail, LANES - i * SHIFT, 1)
        moved = jnp.where(lanes < coeffs - LANES, moved, 0.0)
        parts.append(jnp.concatenate([tiles[i], moved], axis=1).astype(BF))
    return parts


def prepare_kernel(
    batch_class, batch_count, me, group_send, own_ref, ops_hbm, group_ref, far_ref, far_send_ref,
    signs_ref, far_out, group_out, near_ops, rest_ops, ops_buf, low_table, high_table, near_mats,
    rest_mats, stage, in_sems, out_sems,
):
    batches = batch_class.shape[1]
    coeffs, cells = own_ref.shape
    near = near_mats.shape[0]
    group_batches = group_ref.shape[1]
    far_batches = far_ref.shape[1]
    group_slots = group_out.shape[0]
    far_slots = far_out.shape[0] // 4
    chunks = [(at, min(CHUNK, coeffs - at)) for at in range(0, coeffs, CHUNK)]
    copies = [
        pltpu.make_async_copy(
            ops_hbm.at[pl.ds(at, size)], ops_buf.at[pl.ds(at, size)], in_sems.at[i]
        )
        for i, (at, size) in enumerate(chunks)
    ]
    for copy in copies:
        copy.start()

    rows = lax.broadcasted_iota(jnp.int32, (2 * batches, WIDE), 0)
    lanes = lax.broadcasted_iota(jnp.int32, (2 * batches, WIDE), 1)
    wanted = jnp.zeros((2 * batches, WIDE), jnp.int32)
    for i in range(batches):
        wanted = jnp.where(rows == i, batch_class[0, i], wanted)
        wanted = jnp.where(rows == batches + i, batch_class[0, i] + LANES, wanted)
    hot = jnp.where(lanes == wanted, 1.0, 0.0).astype(BF)
    high_table[...] = jnp.zeros(high_table.shape, F32)
    low_table[coeffs * PITCH :, :] = jnp.zeros(((PAD_ROWS - coeffs) * PITCH, LANES), F32)

    signs = signs_ref[...]
    own = padded_rows(own_ref[...])
    own_half = own.astype(BF)
    sign_column = jnp.transpose(jnp.broadcast_to(signs, (LANES, WIDE)))
    flipped = (own * sign_column[:, :cells]).astype(BF)

    def gathered(pairs_ref, count_batches, first_batch, slots):
        counts = []
        for b in range(count_batches):
            hot_t, hot_u = pair_hots(
                pairs_ref, b, batch_count[0, first_batch + b], cells, slots
            )
            counts.append(dot_nt(hot_u, hot_t).astype(BF))
        return dot_nt(jnp.concatenate(counts, axis=0), flipped)

    far_sum = gathered(far_ref, far_batches, near + group_batches, far_slots)
    group_sum = gathered(group_ref, group_batches, near, group_slots)
    far_own = jnp.transpose(dot_nn(own_half, one_hot(far_send_ref[...], cells)))
    row = scalar_row(lambda i: group_send[0, me[0], i // 8, i % 8], group_slots)
    group_own = jnp.transpose(dot_nn(own_half, one_hot(row, cells)))[:group_slots]

    def keep(at, picked):
        low_table[pl.ds(at * PITCH, batches), :] = picked[:, :LANES]
        high_table[pl.ds(at * PITCH, batches), : coeffs - LANES] = picked[:, LANES:]

    for copy, (at, size) in zip(copies, chunks):
        copy.wait()
        for i in range(at, at + size, 2):
            if i + 1 < at + size:
                both = dot_nt(hot, jnp.concatenate([ops_buf[i], ops_buf[i + 1]], axis=1))
                keep(i, both[:batches])
                keep(i + 1, both[batches:])
            else:
                keep(i, dot_nt(hot[:batches, :LANES], ops_buf[i]))

    def matrix(i):
        low = low_table[pl.ds(i, PAD_ROWS, stride=PITCH), :]
        high = high_table[pl.ds(i, PAD_ROWS, stride=PITCH), :]
        return jnp.concatenate([low, high], axis=1).astype(BF)

    for i in range(batches - near):
        rest_mats[i] = matrix(near + i)
    rest_copy = pltpu.make_async_copy(rest_mats, rest_ops, out_sems.at[0])
    rest_copy.start()
    for i in range(near):
        near_mats[i] = matrix(i)
    near_copy = pltpu.make_async_copy(near_mats, near_ops, out_sems.at[1])
    near_copy.start()

    def back_terms(summed, count_batches, first_batch, slots):
        total = jnp.zeros((slots, PAD_ROWS), F32)
        for b in range(count_batches):
            high, low = split(summed[b * slots : (b + 1) * slots])
            both = dot_nt(jnp.concatenate([high, low], axis=0), rest_mats[first_batch + b])
            total = total + both[:slots] + both[slots:]
        total = total * signs[:, :PAD_ROWS]
        total = jnp.concatenate([total, jnp.zeros((slots, WIDE - PAD_ROWS), F32)], axis=1)
        high, low = split(total)
        return high.astype(F32), low.astype(F32)

    tiles = pack_tiles(*back_terms(far_sum, far_batches, group_batches, far_slots), far_own)
    for i in range(4):
        stage[pl.ds(i, far_slots, stride=4), :] = tiles[i]
    far_out[...] = stage[...].astype(BF)
    tiles = pack_tiles(*back_terms(group_sum, group_batches, 0, group_slots), group_own)
    group_out[...] = jnp.concatenate(tiles, axis=1).astype(BF)
    rest_copy.wait()
    near_copy.wait()


def near_kernel(
    batch_count, own_ref, near_ref, group_ref, far_ref, ops_ref, signs_ref, out_ref, counts_ref
):
    cells = own_ref.shape[1]
    near = ops_ref.shape[0]
    signs = signs_ref[...]
    own = padded_rows(own_ref[...])
    own_half = own.astype(BF)
    sign_column = jnp.transpose(jnp.broadcast_to(signs, (LANES, WIDE)))
    flipped = (own * sign_column[:, :cells]).astype(BF)
    forward, backward = [], []
    for b in range(near):
        hot_t, hot_u = pair_hots(near_ref, b, batch_count[0, b], cells, cells)
        forward.append(dot_nt(hot_t, hot_u).astype(BF))
        backward.append(dot_nt(hot_u, hot_t).astype(BF))
    ahead = dot_nt(jnp.concatenate(forward, axis=0), own_half)
    behind = dot_nt(jnp.concatenate(backward, axis=0), flipped)
    total = jnp.zeros((cells, PAD_ROWS), F32)
    mirrored = jnp.zeros((cells, PAD_ROWS), F32)
    for b in range(near):
        part = slice(b * cells, (b + 1) * cells)
        both = dot_nt(
            jnp.concatenate([*split(ahead[part]), *split(behind[part])], axis=0), ops_ref[b]
        )
        total = total + both[:cells] + both[cells : 2 * cells]
        mirrored = mirrored + both[2 * cells : 3 * cells] + both[3 * cells :]
    out_ref[...] = total + mirrored * signs[:, :PAD_ROWS]
    done = near
    for pairs_ref in (group_ref, far_ref):
        for b in range(pairs_ref.shape[1]):
            hot_t, hot_u = pair_hots(pairs_ref, b, batch_count[0, done], cells, LANES)
            counts_ref[done - near] = dot_nt(hot_t, hot_u).astype(BF)
            done += 1


def finish_kernel(
    me, group_send, near_sum, counts_ref, ops_ref, far_send_ref, far_in, group_in, out_ref, stage
):
    coeffs, cells = out_ref.shape
    far_slots = far_in.shape[0] // 4
    group_slots = group_in.shape[0]
    group_batches = counts_ref.shape[0] // 2
    stage[...] = far_in[...].astype(F32)
    tiles = [stage[pl.ds(i, far_slots, stride=4), :] for i in range(4)]
    far_high, far_low, far_arrived = unpack_tiles(tiles, coeffs)
    tiles = [group_in[:, i * LANES : (i + 1) * LANES].astype(F32) for i in range(4)]
    group_high, group_low, group_arrived = unpack_tiles(tiles, coeffs)

    total = near_sum[...]
    for first, arrived in ((0, group_arrived), (group_batches, far_arrived)):
        slots = arrived.shape[0]
        counts = [counts_ref[first + b][:, :slots] for b in range(group_batches)]
        summed = dot_nn(jnp.concatenate(counts, axis=0), arrived)
        for b in range(group_batches):
            high, low = split(summed[b * cells : (b + 1) * cells])
            both = dot_nt(jnp.concatenate([high, low], axis=0), ops_ref[first + b])
            total = total + both[:cells] + both[cells:]

    far_hot = one_hot(far_send_ref[...], cells)
    row = scalar_row(lambda i: group_send[0, me[0], i // 8, i % 8], group_slots)
    group_hot = one_hot(row, cells)[:, :group_slots]
    home = dot_nn(far_hot, far_high) + dot_nn(far_hot, far_low)
    home = home + dot_nn(group_hot, group_high) + dot_nn(group_hot, group_low)
    total = total + home[:, :PAD_ROWS]
    total = jnp.concatenate([total, jnp.zeros((cells, WIDE - PAD_ROWS), F32)], axis=1)
    out_ref[...] = jnp.transpose(total)[:coeffs]


def body(
    multipoles, operators, local_pairs, group_pairs, far_pairs, batch_class, batch_count,
    group_send, far_send,
):
    coeffs, cells = multipoles.shape
    batches = batch_class.shape[1]
    near = local_pairs.shape[1]
    rest = batches - near
    group_size = lax.axis_size("grp")
    ranges = lax.axis_size("cells")
    far_slots = far_send.shape[1] * far_send.shape[2]
    far_send = far_send.reshape(1, far_slots)
    group_slots = group_size * group_send.shape[3]
    me = lax.axis_index("grp").reshape(1)
    signs = jnp.asarray(lane_signs())
    smem = pl.BlockSpec(memory_space=pltpu.SMEM)
    vmem = pl.BlockSpec(memory_space=pltpu.VMEM)
    hbm = pl.BlockSpec(memory_space=pl.ANY)
    chunk_count = -(-coeffs // CHUNK)
    far_rows, group_rows, ops_near, ops_rest = pl.pallas_call(
        prepare_kernel,
        in_specs=[smem] * 4 + [vmem, hbm] + [vmem] * 4,
        out_specs=[vmem, vmem, hbm, hbm],
        out_shape=[
            jax.ShapeDtypeStruct((far_slots * 4, LANES), BF),
            jax.ShapeDtypeStruct((group_slots, 4 * LANES), BF),
            jax.ShapeDtypeStruct((near, PAD_ROWS, WIDE), BF),
            jax.ShapeDtypeStruct((rest, PAD_ROWS, WIDE), BF),
        ],
        scratch_shapes=[
            pltpu.VMEM(operators.shape, BF),
            pltpu.VMEM((PAD_ROWS * PITCH, LANES), F32),
            pltpu.VMEM((PAD_ROWS * PITCH, LANES), F32),
            pltpu.VMEM((near, PAD_ROWS, WIDE), BF),
            pltpu.VMEM((rest, PAD_ROWS, WIDE), BF),
            pltpu.VMEM((far_slots * 4, LANES), F32),
            pltpu.SemaphoreType.DMA((chunk_count,)),
            pltpu.SemaphoreType.DMA((2,)),
        ],
        compiler_params=pltpu.CompilerParams(vmem_limit_bytes=60 * 1024 * 1024),
        name="prepare",
    )(
        batch_class, batch_count, me, group_send, multipoles, operators, group_pairs, far_pairs,
        far_send, signs,
    )
    group_got = lax.all_to_all(
        group_rows.reshape(group_size, -1, 4 * LANES), "grp", split_axis=0, concat_axis=0, tiled=True
    ).reshape(group_rows.shape)
    far_got = lax.all_to_all(
        far_rows.reshape(ranges, -1, LANES), "cells", split_axis=0, concat_axis=0, tiled=True
    ).reshape(far_rows.shape)
    near_sum, counts = pl.pallas_call(
        near_kernel,
        in_specs=[smem] + [vmem] * 6,
        out_specs=[vmem, vmem],
        out_shape=[
            jax.ShapeDtypeStruct((cells, PAD_ROWS), F32),
            jax.ShapeDtypeStruct((rest, cells, LANES), BF),
        ],
        compiler_params=pltpu.CompilerParams(vmem_limit_bytes=24 * 1024 * 1024),
        cost_estimate=pl.CostEstimate(
            flops=20_000_000_000, bytes_accessed=40_000_000, transcendentals=0
        ),
        name="near",
    )(batch_count, multipoles, local_pairs, group_pairs, far_pairs, ops_near, signs)
    return pl.pallas_call(
        finish_kernel,
        in_specs=[smem] * 2 + [vmem] * 6,
        out_specs=vmem,
        out_shape=jax.ShapeDtypeStruct((coeffs, cells), F32),
        scratch_shapes=[pltpu.VMEM((far_slots * 4, LANES), F32)],
        compiler_params=pltpu.CompilerParams(vmem_limit_bytes=24 * 1024 * 1024),
        name="finish",
    )(me, group_send, near_sum, counts, ops_rest, far_send, far_got, group_got)


def solution(mesh):
    placed = (
        P(None, ("cells", "grp")),
        P(),
        P(("cells", "grp"), None, None, None),
        P(("cells", "grp"), None, None, None),
        P(("cells", "grp"), None, None, None),
        P(("cells", "grp"), None),
        P(("cells", "grp"), None),
        P("cells", None, None, None),
        P(("cells", "grp"), None, None),
    )
    return jax.shard_map(
        body, mesh=mesh, in_specs=placed, out_specs=P(None, ("cells", "grp")), check_vma=False
    )
```

```python
import jax
import jax.numpy as jnp
from jax import lax
from jax.experimental import pallas as pl
from jax.experimental.pallas import tpu as pltpu
from jax.sharding import PartitionSpec as P

ORDER = 8
LANES = 128
WIDE = 256
PAD_ROWS = 176
PITCH = 40
CHUNK = 64
SHIFT = 40
MIB = 1024 * 1024
NEAR_LIMIT = 24 * MIB
BF = jnp.bfloat16
F32 = jnp.float32


def signs_of(index):
    degree = jnp.zeros(index.shape, jnp.int32)
    count = 0
    for d in range(ORDER + 1):
        count += (d + 1) * (d + 2) // 2
        degree = degree + jnp.where(index >= count, 1, 0)
    sign = jnp.where(degree % 2 == 0, 1.0, -1.0)
    return jnp.where(index < count, sign, 0.0)


def lane_signs():
    return signs_of(lax.broadcasted_iota(jnp.int32, (1, WIDE), 1))


def own_tables(own):
    own = own.astype(F32)
    own = jnp.concatenate([own, jnp.zeros((WIDE - own.shape[0], own.shape[1]), F32)], axis=0)
    signs = signs_of(lax.broadcasted_iota(jnp.int32, own.shape, 0))
    return own.astype(BF), (own * signs).astype(BF)


def dot_nt(a, b):
    return lax.dot_general(a, b, (((1,), (1,)), ((), ())), preferred_element_type=F32)


def dot_nn(a, b):
    return lax.dot_general(a, b, (((1,), (0,)), ((), ())), preferred_element_type=F32)


def split(x):
    high = x.astype(BF)
    low = (x - high.astype(F32)).astype(BF)
    return high, low


def one_hot(ids, size):
    rows = lax.broadcasted_iota(jnp.int32, (size, ids.shape[1]), 0)
    return jnp.where(rows == ids, 1.0, 0.0).astype(BF)


def pair_hots(pairs_ref, batch, count, first, second):
    targets = pairs_ref[0, batch, 0:1, :]
    sources = pairs_ref[0, batch, 1:2, :]
    spots = lax.broadcasted_iota(jnp.int32, targets.shape, 1)
    targets = jnp.where(spots < count, targets, -1)
    return one_hot(targets, first), one_hot(sources, second)


def scalar_row(read, count):
    lanes = lax.broadcasted_iota(jnp.int32, (1, LANES), 1)
    row = jnp.full((1, LANES), -1, jnp.int32)
    for i in range(count):
        row = jnp.where(lanes == i, read(i), row)
    return row


def pack_tiles(high, low, own):
    tail = high[:, LANES:] + pltpu.roll(low[:, LANES:], SHIFT, 1)
    tail = tail + pltpu.roll(own[:, LANES:], 2 * SHIFT, 1)
    return [high[:, :LANES], low[:, :LANES], own[:, :LANES], tail]


def unpack_tiles(tiles, coeffs):
    tail = tiles[3]
    lanes = lax.broadcasted_iota(jnp.int32, tail.shape, 1)
    parts = []
    for i in range(3):
        moved = tail if i == 0 else pltpu.roll(tail, LANES - i * SHIFT, 1)
        moved = jnp.where(lanes < coeffs - LANES, moved, 0.0)
        parts.append(jnp.concatenate([tiles[i], moved], axis=1).astype(BF))
    return parts


def prepare_kernel(
    me, class_hbm, count_hbm, send_hbm, own_hbm, ops_hbm, group_hbm, far_hbm, far_send_hbm,
    far_out, group_out, near_ops, far_ops, batch_class, batch_count, group_send, own_ref, group_ref,
    far_ref, far_send_ref, ops_buf, low_table, high_table, near_mats, far_mats, stage, small_sems,
    in_sems, out_sems,
):
    batches = batch_class.shape[1]
    coeffs, cells = own_ref.shape
    first_far = near_mats.shape[0]
    group_batches = group_ref.shape[1]
    far_batches = far_ref.shape[1]
    first_group = first_far - group_batches
    group_slots = group_out.shape[0]
    far_slots = far_out.shape[0] // 4
    small = [
        pltpu.make_async_copy(source, target, small_sems.at[i])
        for i, (source, target) in enumerate(
            (
                (class_hbm, batch_class),
                (count_hbm, batch_count),
                (send_hbm, group_send),
                (own_hbm, own_ref),
                (group_hbm, group_ref),
                (far_hbm, far_ref),
                (far_send_hbm, far_send_ref),
            )
        )
    ]
    for copy in small:
        copy.start()
    chunks = [(at, min(CHUNK, coeffs - at)) for at in range(0, coeffs, CHUNK)]
    copies = [
        pltpu.make_async_copy(
            ops_hbm.at[pl.ds(at, size)], ops_buf.at[pl.ds(at, size)], in_sems.at[i]
        )
        for i, (at, size) in enumerate(chunks)
    ]
    for copy in copies:
        copy.start()

    high_table[...] = jnp.zeros(high_table.shape, F32)
    low_table[coeffs * PITCH :, :] = jnp.zeros(((PAD_ROWS - coeffs) * PITCH, LANES), F32)
    for copy in small:
        copy.wait()

    rows = lax.broadcasted_iota(jnp.int32, (2 * batches, WIDE), 0)
    lanes = lax.broadcasted_iota(jnp.int32, (2 * batches, WIDE), 1)
    wanted = jnp.zeros((2 * batches, WIDE), jnp.int32)
    for i in range(batches):
        wanted = jnp.where(rows == i, batch_class[0, i], wanted)
        wanted = jnp.where(rows == batches + i, batch_class[0, i] + LANES, wanted)
    hot = jnp.where(lanes == wanted, 1.0, 0.0).astype(BF)

    own_half, flipped = own_tables(own_ref[...])

    def gathered(pairs_ref, count_batches, first_batch, slots):
        counts = []
        for b in range(count_batches):
            hot_t, hot_u = pair_hots(
                pairs_ref, b, batch_count[0, first_batch + b], cells, slots
            )
            counts.append(dot_nt(hot_u, hot_t).astype(BF))
        return dot_nt(jnp.concatenate(counts, axis=0), flipped)

    far_sum = gathered(far_ref, far_batches, first_far, far_slots)
    group_sum = gathered(group_ref, group_batches, first_group, group_slots)
    far_own = jnp.transpose(dot_nn(own_half, one_hot(far_send_ref[...], cells)))
    row = scalar_row(lambda i: group_send[0, me[0], i // 8, i % 8], group_slots)
    group_own = jnp.transpose(dot_nn(own_half, one_hot(row, cells)))[:group_slots]

    def keep(at, picked):
        low_table[pl.ds(at * PITCH, batches), :] = picked[:, :LANES]
        high_table[pl.ds(at * PITCH, batches), : coeffs - LANES] = picked[:, LANES:]

    outs = []

    def take_out(c):
        at = chunks[c][0]
        size = min(CHUNK, PAD_ROWS - at)
        for i in range(batches):
            low = low_table[pl.ds(at * PITCH + i, size, stride=PITCH), :]
            high = high_table[pl.ds(at * PITCH + i, size, stride=PITCH), :]
            mats, place = (near_mats, i) if i < first_far else (far_mats, i - first_far)
            mats[place, at : at + size, :] = jnp.concatenate([low, high], axis=1).astype(BF)
        for k, (mats, target) in enumerate(((near_mats, near_ops), (far_mats, far_ops))):
            out = pltpu.make_async_copy(
                mats.at[:, pl.ds(at, size), :],
                target.at[:, pl.ds(at, size), :],
                out_sems.at[2 * c + k],
            )
            out.start()
            outs.append(out)

    for c, (copy, (at, size)) in enumerate(zip(copies, chunks)):
        copy.wait()
        for i in range(at, at + size, 2):
            if i + 1 < at + size:
                both = dot_nt(hot, jnp.concatenate([ops_buf[i], ops_buf[i + 1]], axis=1))
                keep(i, both[:batches])
                keep(i + 1, both[batches:])
            else:
                keep(i, dot_nt(hot[:batches, :LANES], ops_buf[i]))
        if c > 0:
            take_out(c - 1)
    take_out(len(chunks) - 1)

    signs = lane_signs()

    def back_terms(summed, mats, count_batches, first, slots):
        total = jnp.zeros((slots, PAD_ROWS), F32)
        for b in range(count_batches):
            high, low = split(summed[b * slots : (b + 1) * slots])
            both = dot_nt(jnp.concatenate([high, low], axis=0), mats[first + b])
            total = total + both[:slots] + both[slots:]
        total = total * signs[:, :PAD_ROWS]
        total = jnp.concatenate([total, jnp.zeros((slots, WIDE - PAD_ROWS), F32)], axis=1)
        high, low = split(total)
        return high.astype(F32), low.astype(F32)

    tiles = pack_tiles(*back_terms(far_sum, far_mats, far_batches, 0, far_slots), far_own)
    for i in range(4):
        stage[pl.ds(i, far_slots, stride=4), :] = tiles[i]
    far_out[...] = stage[...].astype(BF)
    tiles = pack_tiles(
        *back_terms(group_sum, near_mats, group_batches, first_group, group_slots), group_own
    )
    group_out[...] = jnp.concatenate(tiles, axis=1).astype(BF)
    for out in outs:
        out.wait()


def forward_terms(total, counts, arrived, matrix):
    cells = total.shape[0]
    summed = dot_nn(jnp.concatenate(counts, axis=0), arrived)
    for b in range(len(counts)):
        high, low = split(summed[b * cells : (b + 1) * cells])
        both = dot_nt(jnp.concatenate([high, low], axis=0), matrix(b))
        total = total + both[:cells] + both[cells:]
    return total


def near_kernel(
    me, batch_count, group_send, own_ref, near_ref, group_ref, far_ref, group_in, ops_hbm,
    out_ref, counts_ref, ops_ref, sems,
):
    coeffs, cells = own_ref.shape
    near = near_ref.shape[1]
    group_slots = group_in.shape[0]
    parts = sems.shape[0]
    size = ops_hbm.shape[0] // parts
    copies = [
        pltpu.make_async_copy(
            ops_hbm.at[pl.ds(i * size, size)], ops_ref.at[pl.ds(i * size, size)], sems.at[i]
        )
        for i in range(parts)
    ]
    for copy in copies:
        copy.start()
    own_half, flipped = own_tables(own_ref[...])
    forward, backward, remote = [], [], []
    for b in range(near):
        hot_t, hot_u = pair_hots(near_ref, b, batch_count[0, b], cells, cells)
        forward.append(dot_nt(hot_t, hot_u).astype(BF))
        backward.append(dot_nt(hot_u, hot_t).astype(BF))
    ahead = dot_nt(jnp.concatenate(forward, axis=0), own_half)
    behind = dot_nt(jnp.concatenate(backward, axis=0), flipped)
    done = near
    for b in range(group_ref.shape[1]):
        hot_t, hot_u = pair_hots(group_ref, b, batch_count[0, done], cells, group_slots)
        remote.append(dot_nt(hot_t, hot_u).astype(BF))
        done += 1
    for b in range(far_ref.shape[1]):
        hot_t, hot_u = pair_hots(far_ref, b, batch_count[0, done], cells, LANES)
        counts_ref[b] = dot_nt(hot_t, hot_u).astype(BF)
        done += 1
    total = jnp.zeros((cells, PAD_ROWS), F32)
    mirrored = jnp.zeros((cells, PAD_ROWS), F32)
    for b in range(near):
        if b % size == 0:
            copies[b // size].wait()
        part = slice(b * cells, (b + 1) * cells)
        both = dot_nt(
            jnp.concatenate([*split(ahead[part]), *split(behind[part])], axis=0), ops_ref[b]
        )
        total = total + both[:cells] + both[cells : 2 * cells]
        mirrored = mirrored + both[2 * cells : 3 * cells] + both[3 * cells :]
    total = total + mirrored * lane_signs()[:, :PAD_ROWS]
    for copy in copies[-(-near // size) :]:
        copy.wait()
    tiles = [group_in[:, i * LANES : (i + 1) * LANES].astype(F32) for i in range(4)]
    high, low, arrived = unpack_tiles(tiles, coeffs)
    total = forward_terms(total, remote, arrived, lambda b: ops_ref[near + b])
    row = scalar_row(lambda i: group_send[0, me[0], i // 8, i % 8], group_slots)
    hot = one_hot(row, cells)[:, :group_slots]
    out_ref[...] = total + (dot_nn(hot, high) + dot_nn(hot, low))[:, :PAD_ROWS]


def finish_kernel(near_sum, counts_ref, ops_ref, far_send_ref, far_in, out_ref, stage):
    coeffs, cells = out_ref.shape
    far_slots = far_in.shape[0] // 4
    stage[...] = far_in[...].astype(F32)
    tiles = [stage[pl.ds(i, far_slots, stride=4), :] for i in range(4)]
    high, low, arrived = unpack_tiles(tiles, coeffs)
    counts = [counts_ref[b] for b in range(counts_ref.shape[0])]
    total = forward_terms(near_sum[...], counts, arrived, lambda b: ops_ref[b])
    hot = one_hot(far_send_ref[...], cells)
    total = total + (dot_nn(hot, high) + dot_nn(hot, low))[:, :PAD_ROWS]
    total = jnp.concatenate([total, jnp.zeros((cells, WIDE - PAD_ROWS), F32)], axis=1)
    out_ref[...] = jnp.transpose(total)[:coeffs]


def body(
    multipoles, operators, local_pairs, group_pairs, far_pairs, batch_class, batch_count,
    group_send, far_send,
):
    coeffs, cells = multipoles.shape
    batches = batch_class.shape[1]
    far_batches = far_pairs.shape[1]
    first_far = batches - far_batches
    group_size = lax.axis_size("grp")
    ranges = lax.axis_size("cells")
    far_slots = far_send.shape[1] * far_send.shape[2]
    far_send = far_send.reshape(1, far_slots)
    group_slots = group_size * group_send.shape[3]
    me = lax.axis_index("grp").reshape(1)
    smem = pl.BlockSpec(memory_space=pltpu.SMEM)
    vmem = pl.BlockSpec(memory_space=pltpu.VMEM)
    hbm = pl.BlockSpec(memory_space=pl.ANY)
    chunk_count = -(-coeffs // CHUNK)
    far_rows, group_rows, ops_near, ops_far = pl.pallas_call(
        prepare_kernel,
        in_specs=[smem] + [hbm] * 8,
        out_specs=[vmem, vmem, hbm, hbm],
        out_shape=[
            jax.ShapeDtypeStruct((far_slots * 4, LANES), BF),
            jax.ShapeDtypeStruct((group_slots, 4 * LANES), BF),
            jax.ShapeDtypeStruct((first_far, PAD_ROWS, WIDE), BF),
            jax.ShapeDtypeStruct((far_batches, PAD_ROWS, WIDE), BF),
        ],
        scratch_shapes=[
            pltpu.SMEM(batch_class.shape, jnp.int32),
            pltpu.SMEM(batch_count.shape, jnp.int32),
            pltpu.SMEM(group_send.shape, jnp.int32),
            pltpu.VMEM(multipoles.shape, BF),
            pltpu.VMEM(group_pairs.shape, jnp.int32),
            pltpu.VMEM(far_pairs.shape, jnp.int32),
            pltpu.VMEM(far_send.shape, jnp.int32),
            pltpu.VMEM(operators.shape, BF),
            pltpu.VMEM((PAD_ROWS * PITCH, LANES), F32),
            pltpu.VMEM((PAD_ROWS * PITCH, LANES), F32),
            pltpu.VMEM((first_far, PAD_ROWS, WIDE), BF),
            pltpu.VMEM((far_batches, PAD_ROWS, WIDE), BF),
            pltpu.VMEM((far_slots * 4, LANES), F32),
            pltpu.SemaphoreType.DMA((7,)),
            pltpu.SemaphoreType.DMA((chunk_count,)),
            pltpu.SemaphoreType.DMA((2 * chunk_count,)),
        ],
        compiler_params=pltpu.CompilerParams(vmem_limit_bytes=60 * MIB),
        name="prepare",
    )(
        me, batch_class, batch_count, group_send, multipoles, operators, group_pairs, far_pairs,
        far_send,
    )
    group_got = lax.all_to_all(
        group_rows.reshape(group_size, -1, 4 * LANES), "grp", split_axis=0, concat_axis=0, tiled=True
    ).reshape(group_rows.shape)
    far_got = lax.all_to_all(
        far_rows.reshape(ranges, -1, LANES), "cells", split_axis=0, concat_axis=0, tiled=True
    ).reshape(far_rows.shape)
    near_sum, counts = pl.pallas_call(
        near_kernel,
        in_specs=[smem] * 3 + [vmem] * 5 + [hbm],
        out_specs=[vmem, vmem],
        out_shape=[
            jax.ShapeDtypeStruct((cells, PAD_ROWS), F32),
            jax.ShapeDtypeStruct((far_batches, cells, LANES), BF),
        ],
        scratch_shapes=[
            pltpu.VMEM((first_far, PAD_ROWS, WIDE), BF),
            pltpu.SemaphoreType.DMA((3,)),
        ],
        compiler_params=pltpu.CompilerParams(vmem_limit_bytes=NEAR_LIMIT),
        cost_estimate=pl.CostEstimate(
            flops=20_000_000_000, bytes_accessed=40_000_000, transcendentals=0
        ),
        name="near",
    )(
        me, batch_count, group_send, multipoles, local_pairs, group_pairs, far_pairs, group_got,
        ops_near,
    )
    return pl.pallas_call(
        finish_kernel,
        in_specs=[vmem] * 5,
        out_specs=vmem,
        out_shape=jax.ShapeDtypeStruct((coeffs, cells), F32),
        scratch_shapes=[pltpu.VMEM((far_slots * 4, LANES), F32)],
        compiler_params=pltpu.CompilerParams(vmem_limit_bytes=24 * MIB),
        name="finish",
    )(near_sum, counts, ops_far, far_send, far_got)


def solution(mesh):
    placed = (
        P(None, ("cells", "grp")),
        P(),
        P(("cells", "grp"), None, None, None),
        P(("cells", "grp"), None, None, None),
        P(("cells", "grp"), None, None, None),
        P(("cells", "grp"), None),
        P(("cells", "grp"), None),
        P("cells", None, None, None),
        P(("cells", "grp"), None, None),
    )
    return jax.shard_map(
        body, mesh=mesh, in_specs=placed, out_specs=P(None, ("cells", "grp")), check_vma=False
    )
```

```python
import jax
import jax.numpy as jnp
from jax import lax
from jax.experimental import pallas as pl
from jax.experimental.pallas import tpu as pltpu
from jax.sharding import PartitionSpec as P

ORDER = 8
LANES = 128
WIDE = 256
PAD_ROWS = 176
PITCH = 40
CHUNKS = (0, 96)
SHIFT = 40
MIB = 1024 * 1024
BF = jnp.bfloat16
F32 = jnp.float32


def signs_of(index):
    degree = jnp.zeros(index.shape, jnp.int32)
    count = 0
    for d in range(ORDER + 1):
        count += (d + 1) * (d + 2) // 2
        degree = degree + jnp.where(index >= count, 1, 0)
    sign = jnp.where(degree % 2 == 0, 1.0, -1.0)
    return jnp.where(index < count, sign, 0.0)


def lane_signs():
    return signs_of(lax.broadcasted_iota(jnp.int32, (1, WIDE), 1))


def own_tables(own):
    own = own.astype(F32)
    own = jnp.concatenate([own, jnp.zeros((WIDE - own.shape[0], own.shape[1]), F32)], axis=0)
    signs = signs_of(lax.broadcasted_iota(jnp.int32, own.shape, 0))
    return own.astype(BF), (own * signs).astype(BF)


def dot_nt(a, b):
    return lax.dot_general(a, b, (((1,), (1,)), ((), ())), preferred_element_type=F32)


def dot_nn(a, b):
    return lax.dot_general(a, b, (((1,), (0,)), ((), ())), preferred_element_type=F32)


def split(x):
    high = x.astype(BF)
    low = (x - high.astype(F32)).astype(BF)
    return high, low


def one_hot(ids, size):
    rows = lax.broadcasted_iota(jnp.int32, (size, ids.shape[1]), 0)
    return jnp.where(rows == ids, 1.0, 0.0).astype(BF)


def pair_hots(pairs_ref, batch, count, first, second):
    targets = pairs_ref[0, batch, 0:1, :]
    sources = pairs_ref[0, batch, 1:2, :]
    spots = lax.broadcasted_iota(jnp.int32, targets.shape, 1)
    targets = jnp.where(spots < count, targets, -1)
    return one_hot(targets, first), one_hot(sources, second)


def scalar_row(read, count):
    lanes = lax.broadcasted_iota(jnp.int32, (1, LANES), 1)
    row = jnp.full((1, LANES), -1, jnp.int32)
    for i in range(count):
        row = jnp.where(lanes == i, read(i), row)
    return row


def pack_tiles(high, low, own):
    tail = high[:, LANES:] + pltpu.roll(low[:, LANES:], SHIFT, 1)
    tail = tail + pltpu.roll(own[:, LANES:], 2 * SHIFT, 1)
    return [high[:, :LANES], low[:, :LANES], own[:, :LANES], tail]


def unpack_tiles(tiles, coeffs):
    tail = tiles[3]
    lanes = lax.broadcasted_iota(jnp.int32, tail.shape, 1)
    parts = []
    for i in range(3):
        moved = tail if i == 0 else pltpu.roll(tail, LANES - i * SHIFT, 1)
        moved = jnp.where(lanes < coeffs - LANES, moved, 0.0)
        parts.append(jnp.concatenate([tiles[i], moved], axis=1).astype(BF))
    return parts


def prepare_kernel(
    me, class_hbm, count_hbm, send_hbm, own_hbm, ops_hbm, group_hbm, far_hbm, far_send_hbm,
    far_out, group_out, near_ops, rest_ops, batch_class, batch_count, group_send, own_ref, group_ref,
    far_ref, far_send_ref, ops_buf, low_table, high_table, near_mats, rest_mats, stage, small_sems,
    in_sems, out_sems,
):
    batches = batch_class.shape[1]
    coeffs, cells = own_ref.shape
    near = near_mats.shape[0]
    group_batches = group_ref.shape[1]
    far_batches = far_ref.shape[1]
    group_slots = group_out.shape[0]
    far_slots = far_out.shape[0] // 4
    small = [
        pltpu.make_async_copy(source, target, small_sems.at[i])
        for i, (source, target) in enumerate(
            (
                (class_hbm, batch_class),
                (count_hbm, batch_count),
                (send_hbm, group_send),
                (own_hbm, own_ref),
                (group_hbm, group_ref),
                (far_hbm, far_ref),
                (far_send_hbm, far_send_ref),
            )
        )
    ]
    for copy in small:
        copy.start()
    starts = [at for at in CHUNKS if at < coeffs] + [coeffs]
    chunks = [(at, end - at) for at, end in zip(starts, starts[1:])]
    copies = [
        pltpu.make_async_copy(
            ops_hbm.at[pl.ds(at, size)], ops_buf.at[pl.ds(at, size)], in_sems.at[i]
        )
        for i, (at, size) in enumerate(chunks)
    ]
    for copy in copies:
        copy.start()

    high_table[...] = jnp.zeros(high_table.shape, F32)
    low_table[coeffs * PITCH :, :] = jnp.zeros(((PAD_ROWS - coeffs) * PITCH, LANES), F32)
    for copy in small:
        copy.wait()

    rows = lax.broadcasted_iota(jnp.int32, (2 * batches, WIDE), 0)
    lanes = lax.broadcasted_iota(jnp.int32, (2 * batches, WIDE), 1)
    wanted = jnp.zeros((2 * batches, WIDE), jnp.int32)
    for i in range(batches):
        wanted = jnp.where(rows == i, batch_class[0, i], wanted)
        wanted = jnp.where(rows == batches + i, batch_class[0, i] + LANES, wanted)
    hot = jnp.where(lanes == wanted, 1.0, 0.0).astype(BF)

    own_half, flipped = own_tables(own_ref[...])

    def gathered(pairs_ref, count_batches, first_batch, slots):
        counts = []
        for b in range(count_batches):
            hot_t, hot_u = pair_hots(
                pairs_ref, b, batch_count[0, first_batch + b], cells, slots
            )
            counts.append(dot_nt(hot_u, hot_t).astype(BF))
        return dot_nt(jnp.concatenate(counts, axis=0), flipped)

    far_sum = gathered(far_ref, far_batches, near + group_batches, far_slots)
    group_sum = gathered(group_ref, group_batches, near, group_slots)
    far_own = jnp.transpose(dot_nn(own_half, one_hot(far_send_ref[...], cells)))
    row = scalar_row(lambda i: group_send[0, me[0], i // 8, i % 8], group_slots)
    group_own = jnp.transpose(dot_nn(own_half, one_hot(row, cells)))[:group_slots]

    def keep(at, picked):
        low_table[pl.ds(at * PITCH, batches), :] = picked[:, :LANES]
        high_table[pl.ds(at * PITCH, batches), : coeffs - LANES] = picked[:, LANES:]

    outs = []

    def take_out(c):
        at = chunks[c][0]
        size = (chunks[c + 1][0] if c + 1 < len(chunks) else PAD_ROWS) - at
        for i in range(batches):
            low = low_table[pl.ds(at * PITCH + i, size, stride=PITCH), :]
            high = high_table[pl.ds(at * PITCH + i, size, stride=PITCH), :]
            mats, place = (near_mats, i) if i < near else (rest_mats, i - near)
            mats[place, at : at + size, :] = jnp.concatenate([low, high], axis=1).astype(BF)

    def send_out(c):
        at = chunks[c][0]
        size = (chunks[c + 1][0] if c + 1 < len(chunks) else PAD_ROWS) - at
        for k, (mats, target) in enumerate(((near_mats, near_ops), (rest_mats, rest_ops))):
            out = pltpu.make_async_copy(
                mats.at[:, pl.ds(at, size), :],
                target.at[:, pl.ds(at, size), :],
                out_sems.at[2 * c + k],
            )
            out.start()
            outs.append(out)

    for c, (copy, (at, size)) in enumerate(zip(copies, chunks)):
        copy.wait()
        for i in range(at, at + size, 2):
            if i + 1 < at + size:
                both = dot_nt(hot, jnp.concatenate([ops_buf[i], ops_buf[i + 1]], axis=1))
                keep(i, both[:batches])
                keep(i + 1, both[batches:])
            else:
                keep(i, dot_nt(hot[:batches, :LANES], ops_buf[i]))
        if c > 0:
            take_out(c - 1)
            send_out(c - 1)
    take_out(len(chunks) - 1)

    signs = lane_signs()

    def back_terms(summed, count_batches, first, slots):
        total = jnp.zeros((slots, PAD_ROWS), F32)
        for b in range(count_batches):
            high, low = split(summed[b * slots : (b + 1) * slots])
            both = dot_nt(jnp.concatenate([high, low], axis=0), rest_mats[first + b])
            total = total + both[:slots] + both[slots:]
        total = total * signs[:, :PAD_ROWS]
        total = jnp.concatenate([total, jnp.zeros((slots, WIDE - PAD_ROWS), F32)], axis=1)
        high, low = split(total)
        return high.astype(F32), low.astype(F32)

    far_pair = back_terms(far_sum, far_batches, group_batches, far_slots)
    group_pair = back_terms(group_sum, group_batches, 0, group_slots)
    send_out(len(chunks) - 1)
    tiles = pack_tiles(*far_pair, far_own)
    for i in range(4):
        stage[pl.ds(i, far_slots, stride=4), :] = tiles[i]
    far_out[...] = stage[...].astype(BF)
    tiles = pack_tiles(*group_pair, group_own)
    group_out[...] = jnp.concatenate(tiles, axis=1).astype(BF)
    for out in outs:
        out.wait()


def forward_terms(total, counts, arrived, matrix):
    cells = total.shape[0]
    summed = dot_nn(jnp.concatenate(counts, axis=0), arrived)
    for b in range(len(counts)):
        high, low = split(summed[b * cells : (b + 1) * cells])
        both = dot_nt(jnp.concatenate([high, low], axis=0), matrix(b))
        total = total + both[:cells] + both[cells:]
    return total


def near_kernel(
    batch_count, own_ref, near_ref, group_ref, far_ref, ops_ref, out_ref, counts_ref
):
    cells = own_ref.shape[1]
    near = ops_ref.shape[0]
    own_half, flipped = own_tables(own_ref[...])
    forward, backward = [], []
    for b in range(near):
        hot_t, hot_u = pair_hots(near_ref, b, batch_count[0, b], cells, cells)
        forward.append(dot_nt(hot_t, hot_u).astype(BF))
        backward.append(dot_nt(hot_u, hot_t).astype(BF))
    ahead = dot_nt(jnp.concatenate(forward, axis=0), own_half)
    behind = dot_nt(jnp.concatenate(backward, axis=0), flipped)
    total = jnp.zeros((cells, PAD_ROWS), F32)
    mirrored = jnp.zeros((cells, PAD_ROWS), F32)
    for b in range(near):
        part = slice(b * cells, (b + 1) * cells)
        both = dot_nt(
            jnp.concatenate([*split(ahead[part]), *split(behind[part])], axis=0), ops_ref[b]
        )
        total = total + both[:cells] + both[cells : 2 * cells]
        mirrored = mirrored + both[2 * cells : 3 * cells] + both[3 * cells :]
    out_ref[...] = total + mirrored * lane_signs()[:, :PAD_ROWS]
    done = near
    for pairs_ref in (group_ref, far_ref):
        for b in range(pairs_ref.shape[1]):
            hot_t, hot_u = pair_hots(pairs_ref, b, batch_count[0, done], cells, LANES)
            counts_ref[done - near] = dot_nt(hot_t, hot_u).astype(BF)
            done += 1


def finish_kernel(
    me, group_send, near_sum, counts_ref, ops_ref, far_send_ref, far_in, group_in, out_ref, stage
):
    coeffs, cells = out_ref.shape
    far_slots = far_in.shape[0] // 4
    group_slots = group_in.shape[0]
    group_batches = counts_ref.shape[0] // 2
    stage[...] = far_in[...].astype(F32)
    tiles = [stage[pl.ds(i, far_slots, stride=4), :] for i in range(4)]
    far_high, far_low, far_arrived = unpack_tiles(tiles, coeffs)
    tiles = [group_in[:, i * LANES : (i + 1) * LANES].astype(F32) for i in range(4)]
    group_high, group_low, group_arrived = unpack_tiles(tiles, coeffs)
    total = near_sum[...]
    for first, arrived in ((0, group_arrived), (group_batches, far_arrived)):
        counts = [counts_ref[first + b][:, : arrived.shape[0]] for b in range(group_batches)]
        total = forward_terms(total, counts, arrived, lambda b, first=first: ops_ref[first + b])
    far_hot = one_hot(far_send_ref[...], cells)
    row = scalar_row(lambda i: group_send[0, me[0], i // 8, i % 8], group_slots)
    group_hot = one_hot(row, cells)[:, :group_slots]
    home = dot_nn(far_hot, far_high) + dot_nn(far_hot, far_low)
    home = home + dot_nn(group_hot, group_high) + dot_nn(group_hot, group_low)
    total = total + home[:, :PAD_ROWS]
    total = jnp.concatenate([total, jnp.zeros((cells, WIDE - PAD_ROWS), F32)], axis=1)
    out_ref[...] = jnp.transpose(total)[:coeffs]


def body(
    multipoles, operators, local_pairs, group_pairs, far_pairs, batch_class, batch_count,
    group_send, far_send,
):
    coeffs, cells = multipoles.shape
    batches = batch_class.shape[1]
    near = local_pairs.shape[1]
    rest = batches - near
    group_size = lax.axis_size("grp")
    ranges = lax.axis_size("cells")
    far_slots = far_send.shape[1] * far_send.shape[2]
    far_send = far_send.reshape(1, far_slots)
    group_slots = group_size * group_send.shape[3]
    me = lax.axis_index("grp").reshape(1)
    smem = pl.BlockSpec(memory_space=pltpu.SMEM)
    vmem = pl.BlockSpec(memory_space=pltpu.VMEM)
    hbm = pl.BlockSpec(memory_space=pl.ANY)
    chunk_count = len(CHUNKS)
    far_rows, group_rows, ops_near, ops_rest = pl.pallas_call(
        prepare_kernel,
        in_specs=[smem] + [hbm] * 8,
        out_specs=[vmem, vmem, hbm, hbm],
        out_shape=[
            jax.ShapeDtypeStruct((far_slots * 4, LANES), BF),
            jax.ShapeDtypeStruct((group_slots, 4 * LANES), BF),
            jax.ShapeDtypeStruct((near, PAD_ROWS, WIDE), BF),
            jax.ShapeDtypeStruct((rest, PAD_ROWS, WIDE), BF),
        ],
        scratch_shapes=[
            pltpu.SMEM(batch_class.shape, jnp.int32),
            pltpu.SMEM(batch_count.shape, jnp.int32),
            pltpu.SMEM(group_send.shape, jnp.int32),
            pltpu.VMEM(multipoles.shape, BF),
            pltpu.VMEM(group_pairs.shape, jnp.int32),
            pltpu.VMEM(far_pairs.shape, jnp.int32),
            pltpu.VMEM(far_send.shape, jnp.int32),
            pltpu.VMEM(operators.shape, BF),
            pltpu.VMEM((PAD_ROWS * PITCH, LANES), F32),
            pltpu.VMEM((PAD_ROWS * PITCH, LANES), F32),
            pltpu.VMEM((near, PAD_ROWS, WIDE), BF),
            pltpu.VMEM((rest, PAD_ROWS, WIDE), BF),
            pltpu.VMEM((far_slots * 4, LANES), F32),
            pltpu.SemaphoreType.DMA((7,)),
            pltpu.SemaphoreType.DMA((chunk_count,)),
            pltpu.SemaphoreType.DMA((2 * chunk_count,)),
        ],
        compiler_params=pltpu.CompilerParams(vmem_limit_bytes=60 * MIB),
        name="prepare",
    )(
        me, batch_class, batch_count, group_send, multipoles, operators, group_pairs, far_pairs,
        far_send,
    )
    group_got = lax.all_to_all(
        group_rows.reshape(group_size, -1, 4 * LANES), "grp", split_axis=0, concat_axis=0, tiled=True
    ).reshape(group_rows.shape)
    near_sum, counts = pl.pallas_call(
        near_kernel,
        in_specs=[smem] + [vmem] * 5,
        out_specs=[vmem, vmem],
        out_shape=[
            jax.ShapeDtypeStruct((cells, PAD_ROWS), F32),
            jax.ShapeDtypeStruct((rest, cells, LANES), BF),
        ],
        compiler_params=pltpu.CompilerParams(vmem_limit_bytes=24 * MIB),
        cost_estimate=pl.CostEstimate(
            flops=20_000_000_000, bytes_accessed=40_000_000, transcendentals=0
        ),
        name="near",
    )(batch_count, multipoles, local_pairs, group_pairs, far_pairs, ops_near)
    far_rows, near_sum = lax.optimization_barrier((far_rows, near_sum))
    far_got = lax.all_to_all(
        far_rows.reshape(ranges, -1, LANES), "cells", split_axis=0, concat_axis=0, tiled=True
    ).reshape(far_rows.shape)
    return pl.pallas_call(
        finish_kernel,
        in_specs=[smem] * 2 + [vmem] * 6,
        out_specs=vmem,
        out_shape=jax.ShapeDtypeStruct((coeffs, cells), F32),
        scratch_shapes=[pltpu.VMEM((far_slots * 4, LANES), F32)],
        compiler_params=pltpu.CompilerParams(vmem_limit_bytes=24 * MIB),
        name="finish",
    )(me, group_send, near_sum, counts, ops_rest, far_send, far_got, group_got)


def solution(mesh):
    placed = (
        P(None, ("cells", "grp")),
        P(),
        P(("cells", "grp"), None, None, None),
        P(("cells", "grp"), None, None, None),
        P(("cells", "grp"), None, None, None),
        P(("cells", "grp"), None),
        P(("cells", "grp"), None),
        P("cells", None, None, None),
        P(("cells", "grp"), None, None),
    )
    return jax.shard_map(
        body, mesh=mesh, in_specs=placed, out_specs=P(None, ("cells", "grp")), check_vma=False
    )
```

```python
import jax
import jax.numpy as jnp
from jax import lax
from jax.experimental import pallas as pl
from jax.experimental.pallas import tpu as pltpu
from jax.sharding import PartitionSpec as P

ORDER = 8
LANES = 128
WIDE = 256
PAD_ROWS = 176
PITCH = 40
CHUNKS = (0, 96)
SHIFT = 40
MIB = 1024 * 1024
BF = jnp.bfloat16
F32 = jnp.float32


def signs_of(index):
    degree = jnp.zeros(index.shape, jnp.int32)
    count = 0
    for d in range(ORDER + 1):
        count += (d + 1) * (d + 2) // 2
        degree = degree + jnp.where(index >= count, 1, 0)
    sign = jnp.where(degree % 2 == 0, 1.0, -1.0)
    return jnp.where(index < count, sign, 0.0)


def lane_signs():
    return signs_of(lax.broadcasted_iota(jnp.int32, (1, WIDE), 1))


def own_tables(own):
    own = own.astype(F32)
    own = jnp.concatenate([own, jnp.zeros((WIDE - own.shape[0], own.shape[1]), F32)], axis=0)
    signs = signs_of(lax.broadcasted_iota(jnp.int32, own.shape, 0))
    return own.astype(BF), (own * signs).astype(BF)


def dot_nt(a, b):
    return lax.dot_general(a, b, (((1,), (1,)), ((), ())), preferred_element_type=F32)


def dot_nn(a, b):
    return lax.dot_general(a, b, (((1,), (0,)), ((), ())), preferred_element_type=F32)


def split(x):
    high = x.astype(BF)
    low = (x - high.astype(F32)).astype(BF)
    return high, low


def one_hot(ids, size):
    rows = lax.broadcasted_iota(jnp.int32, (size, ids.shape[1]), 0)
    return jnp.where(rows == ids, 1.0, 0.0).astype(BF)


def pair_hots(pairs_ref, batch, count, first, second):
    targets = pairs_ref[0, batch, 0:1, :]
    sources = pairs_ref[0, batch, 1:2, :]
    spots = lax.broadcasted_iota(jnp.int32, targets.shape, 1)
    targets = jnp.where(spots < count, targets, -1)
    return one_hot(targets, first), one_hot(sources, second)


def scalar_row(read, count):
    lanes = lax.broadcasted_iota(jnp.int32, (1, LANES), 1)
    row = jnp.full((1, LANES), -1, jnp.int32)
    for i in range(count):
        row = jnp.where(lanes == i, read(i), row)
    return row


def pack_tiles(high, low, own):
    tail = high[:, LANES:] + pltpu.roll(low[:, LANES:], SHIFT, 1)
    tail = tail + pltpu.roll(own[:, LANES:], 2 * SHIFT, 1)
    return [high[:, :LANES], low[:, :LANES], own[:, :LANES], tail]


def unpack_tiles(tiles, coeffs):
    tail = tiles[3]
    lanes = lax.broadcasted_iota(jnp.int32, tail.shape, 1)
    parts = []
    for i in range(3):
        moved = tail if i == 0 else pltpu.roll(tail, LANES - i * SHIFT, 1)
        moved = jnp.where(lanes < coeffs - LANES, moved, 0.0)
        parts.append(jnp.concatenate([tiles[i], moved], axis=1).astype(BF))
    return parts


def prepare_kernel(
    me, class_hbm, count_hbm, send_hbm, own_hbm, ops_hbm, group_hbm, far_hbm, far_send_hbm,
    far_out, group_out, near_ops, far_ops, batch_class, batch_count, group_send, own_ref, group_ref,
    far_ref, far_send_ref, ops_buf, low_table, high_table, near_mats, far_mats, stage, small_sems,
    in_sems, out_sems,
):
    batches = batch_class.shape[1]
    coeffs, cells = own_ref.shape
    first_far = near_mats.shape[0]
    group_batches = group_ref.shape[1]
    far_batches = far_ref.shape[1]
    first_group = first_far - group_batches
    group_slots = group_out.shape[0]
    far_slots = far_out.shape[0] // 4
    small = [
        pltpu.make_async_copy(source, target, small_sems.at[i])
        for i, (source, target) in enumerate(
            (
                (class_hbm, batch_class),
                (count_hbm, batch_count),
                (send_hbm, group_send),
                (own_hbm, own_ref),
                (group_hbm, group_ref),
                (far_hbm, far_ref),
                (far_send_hbm, far_send_ref),
            )
        )
    ]
    for copy in small:
        copy.start()
    starts = [at for at in CHUNKS if at < coeffs] + [coeffs]
    chunks = [(at, end - at) for at, end in zip(starts, starts[1:])]
    copies = [
        pltpu.make_async_copy(
            ops_hbm.at[pl.ds(at, size)], ops_buf.at[pl.ds(at, size)], in_sems.at[i]
        )
        for i, (at, size) in enumerate(chunks)
    ]
    for copy in copies:
        copy.start()

    high_table[...] = jnp.zeros(high_table.shape, F32)
    low_table[coeffs * PITCH :, :] = jnp.zeros(((PAD_ROWS - coeffs) * PITCH, LANES), F32)
    for copy in small:
        copy.wait()

    rows = lax.broadcasted_iota(jnp.int32, (2 * batches, WIDE), 0)
    lanes = lax.broadcasted_iota(jnp.int32, (2 * batches, WIDE), 1)
    wanted = jnp.zeros((2 * batches, WIDE), jnp.int32)
    for i in range(batches):
        wanted = jnp.where(rows == i, batch_class[0, i], wanted)
        wanted = jnp.where(rows == batches + i, batch_class[0, i] + LANES, wanted)
    hot = jnp.where(lanes == wanted, 1.0, 0.0).astype(BF)

    own_half, flipped = own_tables(own_ref[...])

    def gathered(pairs_ref, count_batches, first_batch, slots):
        counts = []
        for b in range(count_batches):
            hot_t, hot_u = pair_hots(
                pairs_ref, b, batch_count[0, first_batch + b], cells, slots
            )
            counts.append(dot_nt(hot_u, hot_t).astype(BF))
        return dot_nt(jnp.concatenate(counts, axis=0), flipped)

    far_sum = gathered(far_ref, far_batches, first_far, far_slots)
    group_sum = gathered(group_ref, group_batches, first_group, group_slots)
    far_own = jnp.transpose(dot_nn(own_half, one_hot(far_send_ref[...], cells)))
    row = scalar_row(lambda i: group_send[0, me[0], i // 8, i % 8], group_slots)
    group_own = jnp.transpose(dot_nn(own_half, one_hot(row, cells)))[:group_slots]

    def keep(at, picked):
        low_table[pl.ds(at * PITCH, batches), :] = picked[:, :LANES]
        high_table[pl.ds(at * PITCH, batches), : coeffs - LANES] = picked[:, LANES:]

    outs = []

    def take_out(c):
        at = chunks[c][0]
        size = (chunks[c + 1][0] if c + 1 < len(chunks) else PAD_ROWS) - at
        for i in range(batches):
            low = low_table[pl.ds(at * PITCH + i, size, stride=PITCH), :]
            high = high_table[pl.ds(at * PITCH + i, size, stride=PITCH), :]
            mats, place = (near_mats, i) if i < first_far else (far_mats, i - first_far)
            mats[place, at : at + size, :] = jnp.concatenate([low, high], axis=1).astype(BF)

    def send_out(c):
        at = chunks[c][0]
        size = (chunks[c + 1][0] if c + 1 < len(chunks) else PAD_ROWS) - at
        for k, (mats, target) in enumerate(((near_mats, near_ops), (far_mats, far_ops))):
            out = pltpu.make_async_copy(
                mats.at[:, pl.ds(at, size), :],
                target.at[:, pl.ds(at, size), :],
                out_sems.at[2 * c + k],
            )
            out.start()
            outs.append(out)

    for c, (copy, (at, size)) in enumerate(zip(copies, chunks)):
        copy.wait()
        for i in range(at, at + size, 2):
            if i + 1 < at + size:
                both = dot_nt(hot, jnp.concatenate([ops_buf[i], ops_buf[i + 1]], axis=1))
                keep(i, both[:batches])
                keep(i + 1, both[batches:])
            else:
                keep(i, dot_nt(hot[:batches, :LANES], ops_buf[i]))
        if c > 0:
            take_out(c - 1)
            send_out(c - 1)
    take_out(len(chunks) - 1)

    signs = lane_signs()

    def back_terms(summed, mats, count_batches, first, slots):
        total = jnp.zeros((slots, PAD_ROWS), F32)
        for b in range(count_batches):
            high, low = split(summed[b * slots : (b + 1) * slots])
            both = dot_nt(jnp.concatenate([high, low], axis=0), mats[first + b])
            total = total + both[:slots] + both[slots:]
        total = total * signs[:, :PAD_ROWS]
        total = jnp.concatenate([total, jnp.zeros((slots, WIDE - PAD_ROWS), F32)], axis=1)
        high, low = split(total)
        return high.astype(F32), low.astype(F32)

    far_pair = back_terms(far_sum, far_mats, far_batches, 0, far_slots)
    group_pair = back_terms(group_sum, near_mats, group_batches, first_group, group_slots)
    send_out(len(chunks) - 1)
    tiles = pack_tiles(*far_pair, far_own)
    for i in range(4):
        stage[pl.ds(i, far_slots, stride=4), :] = tiles[i]
    far_out[...] = stage[...].astype(BF)
    tiles = pack_tiles(*group_pair, group_own)
    group_out[...] = jnp.concatenate(tiles, axis=1).astype(BF)
    for out in outs:
        out.wait()


def forward_terms(total, counts, arrived, matrix):
    cells = total.shape[0]
    summed = dot_nn(jnp.concatenate(counts, axis=0), arrived)
    for b in range(len(counts)):
        high, low = split(summed[b * cells : (b + 1) * cells])
        both = dot_nt(jnp.concatenate([high, low], axis=0), matrix(b))
        total = total + both[:cells] + both[cells:]
    return total


def count_kernel(batch_count, near_ref, group_ref, far_ref, near_counts, group_counts, far_counts):
    near = near_ref.shape[1]
    cells = near_counts.shape[1]
    for b in range(near):
        hot_t, hot_u = pair_hots(near_ref, b, batch_count[0, b], cells, cells)
        near_counts[b] = dot_nt(hot_t, hot_u).astype(BF)
        near_counts[near + b] = dot_nt(hot_u, hot_t).astype(BF)
    done = near
    for pairs_ref, counts_ref in ((group_ref, group_counts), (far_ref, far_counts)):
        for b in range(pairs_ref.shape[1]):
            hot_t, hot_u = pair_hots(pairs_ref, b, batch_count[0, done], cells, LANES)
            counts_ref[b] = dot_nt(hot_t, hot_u).astype(BF)
            done += 1


def near_kernel(
    me, group_send, own_ref, near_counts, group_counts, group_in, ops_ref, out_ref
):
    coeffs, cells = own_ref.shape
    near = near_counts.shape[0] // 2
    group_slots = group_in.shape[0]
    own_half, flipped = own_tables(own_ref[...])
    ahead = dot_nt(jnp.concatenate([near_counts[b] for b in range(near)], axis=0), own_half)
    behind = dot_nt(jnp.concatenate([near_counts[near + b] for b in range(near)], axis=0), flipped)
    total = jnp.zeros((cells, PAD_ROWS), F32)
    mirrored = jnp.zeros((cells, PAD_ROWS), F32)
    for b in range(near):
        part = slice(b * cells, (b + 1) * cells)
        both = dot_nt(
            jnp.concatenate([*split(ahead[part]), *split(behind[part])], axis=0), ops_ref[b]
        )
        total = total + both[:cells] + both[cells : 2 * cells]
        mirrored = mirrored + both[2 * cells : 3 * cells] + both[3 * cells :]
    total = total + mirrored * lane_signs()[:, :PAD_ROWS]
    tiles = [group_in[:, i * LANES : (i + 1) * LANES].astype(F32) for i in range(4)]
    high, low, arrived = unpack_tiles(tiles, coeffs)
    remote = [group_counts[b][:, :group_slots] for b in range(group_counts.shape[0])]
    total = forward_terms(total, remote, arrived, lambda b: ops_ref[near + b])
    row = scalar_row(lambda i: group_send[0, me[0], i // 8, i % 8], group_slots)
    hot = one_hot(row, cells)[:, :group_slots]
    out_ref[...] = total + (dot_nn(hot, high) + dot_nn(hot, low))[:, :PAD_ROWS]


def finish_kernel(near_sum, counts_ref, ops_ref, far_send_ref, far_in, out_ref, stage):
    coeffs, cells = out_ref.shape
    far_slots = far_in.shape[0] // 4
    stage[...] = far_in[...].astype(F32)
    tiles = [stage[pl.ds(i, far_slots, stride=4), :] for i in range(4)]
    high, low, arrived = unpack_tiles(tiles, coeffs)
    counts = [counts_ref[b] for b in range(counts_ref.shape[0])]
    total = forward_terms(near_sum[...], counts, arrived, lambda b: ops_ref[b])
    hot = one_hot(far_send_ref[...], cells)
    total = total + (dot_nn(hot, high) + dot_nn(hot, low))[:, :PAD_ROWS]
    total = jnp.concatenate([total, jnp.zeros((cells, WIDE - PAD_ROWS), F32)], axis=1)
    out_ref[...] = jnp.transpose(total)[:coeffs]


def body(
    multipoles, operators, local_pairs, group_pairs, far_pairs, batch_class, batch_count,
    group_send, far_send,
):
    coeffs, cells = multipoles.shape
    batches = batch_class.shape[1]
    far_batches = far_pairs.shape[1]
    first_far = batches - far_batches
    group_size = lax.axis_size("grp")
    ranges = lax.axis_size("cells")
    far_slots = far_send.shape[1] * far_send.shape[2]
    far_send = far_send.reshape(1, far_slots)
    group_slots = group_size * group_send.shape[3]
    me = lax.axis_index("grp").reshape(1)
    smem = pl.BlockSpec(memory_space=pltpu.SMEM)
    vmem = pl.BlockSpec(memory_space=pltpu.VMEM)
    hbm = pl.BlockSpec(memory_space=pl.ANY)
    chunk_count = len(CHUNKS)
    far_rows, group_rows, ops_near, ops_far = pl.pallas_call(
        prepare_kernel,
        in_specs=[smem] + [hbm] * 8,
        out_specs=[vmem, vmem, hbm, hbm],
        out_shape=[
            jax.ShapeDtypeStruct((far_slots * 4, LANES), BF),
            jax.ShapeDtypeStruct((group_slots, 4 * LANES), BF),
            jax.ShapeDtypeStruct((first_far, PAD_ROWS, WIDE), BF),
            jax.ShapeDtypeStruct((far_batches, PAD_ROWS, WIDE), BF),
        ],
        scratch_shapes=[
            pltpu.SMEM(batch_class.shape, jnp.int32),
            pltpu.SMEM(batch_count.shape, jnp.int32),
            pltpu.SMEM(group_send.shape, jnp.int32),
            pltpu.VMEM(multipoles.shape, BF),
            pltpu.VMEM(group_pairs.shape, jnp.int32),
            pltpu.VMEM(far_pairs.shape, jnp.int32),
            pltpu.VMEM(far_send.shape, jnp.int32),
            pltpu.VMEM(operators.shape, BF),
            pltpu.VMEM((PAD_ROWS * PITCH, LANES), F32),
            pltpu.VMEM((PAD_ROWS * PITCH, LANES), F32),
            pltpu.VMEM((first_far, PAD_ROWS, WIDE), BF),
            pltpu.VMEM((far_batches, PAD_ROWS, WIDE), BF),
            pltpu.VMEM((far_slots * 4, LANES), F32),
            pltpu.SemaphoreType.DMA((7,)),
            pltpu.SemaphoreType.DMA((chunk_count,)),
            pltpu.SemaphoreType.DMA((2 * chunk_count,)),
        ],
        compiler_params=pltpu.CompilerParams(vmem_limit_bytes=60 * MIB),
        name="prepare",
    )(
        me, batch_class, batch_count, group_send, multipoles, operators, group_pairs, far_pairs,
        far_send,
    )
    group_got = lax.all_to_all(
        group_rows.reshape(group_size, -1, 4 * LANES), "grp", split_axis=0, concat_axis=0, tiled=True
    ).reshape(group_rows.shape)
    counts_shape = (cells, LANES)
    near_counts, group_counts, far_counts = pl.pallas_call(
        count_kernel,
        in_specs=[smem] + [vmem] * 3,
        out_specs=[vmem] * 3,
        out_shape=[
            jax.ShapeDtypeStruct((n,) + counts_shape, BF)
            for n in (2 * local_pairs.shape[1], group_pairs.shape[1], far_batches)
        ],
        compiler_params=pltpu.CompilerParams(vmem_limit_bytes=60 * MIB),
        cost_estimate=pl.CostEstimate(
            flops=10_000_000_000, bytes_accessed=20_000_000, transcendentals=0
        ),
        name="count",
    )(batch_count, local_pairs, group_pairs, far_pairs)
    far_rows, near_counts = lax.optimization_barrier((far_rows, near_counts))
    far_got = lax.all_to_all(
        far_rows.reshape(ranges, -1, LANES), "cells", split_axis=0, concat_axis=0, tiled=True
    ).reshape(far_rows.shape)
    near_sum = pl.pallas_call(
        near_kernel,
        in_specs=[smem, smem] + [vmem] * 5,
        out_specs=vmem,
        out_shape=jax.ShapeDtypeStruct((cells, PAD_ROWS), F32),
        compiler_params=pltpu.CompilerParams(vmem_limit_bytes=24 * MIB),
        cost_estimate=pl.CostEstimate(
            flops=20_000_000_000, bytes_accessed=40_000_000, transcendentals=0
        ),
        name="near",
    )(me, group_send, multipoles, near_counts, group_counts, group_got, ops_near)
    return pl.pallas_call(
        finish_kernel,
        in_specs=[vmem] * 5,
        out_specs=vmem,
        out_shape=jax.ShapeDtypeStruct((coeffs, cells), F32),
        scratch_shapes=[pltpu.VMEM((far_slots * 4, LANES), F32)],
        compiler_params=pltpu.CompilerParams(vmem_limit_bytes=24 * MIB),
        name="finish",
    )(near_sum, far_counts, ops_far, far_send, far_got)


def solution(mesh):
    placed = (
        P(None, ("cells", "grp")),
        P(),
        P(("cells", "grp"), None, None, None),
        P(("cells", "grp"), None, None, None),
        P(("cells", "grp"), None, None, None),
        P(("cells", "grp"), None),
        P(("cells", "grp"), None),
        P("cells", None, None, None),
        P(("cells", "grp"), None, None),
    )
    return jax.shard_map(
        body, mesh=mesh, in_specs=placed, out_specs=P(None, ("cells", "grp")), check_vma=False
    )
```

```python
import jax
import jax.numpy as jnp
from jax import lax
from jax.experimental import pallas as pl
from jax.experimental.pallas import tpu as pltpu
from jax.sharding import PartitionSpec as P

ORDER = 8
LANES = 128
WIDE = 256
PAD_ROWS = 176
PITCH = 40
CHUNKS = (0, 96)
SHIFT = 40
MIB = 1024 * 1024
NEAR_LIMIT = 24 * MIB
BF = jnp.bfloat16
F32 = jnp.float32


def signs_of(index):
    degree = jnp.zeros(index.shape, jnp.int32)
    count = 0
    for d in range(ORDER + 1):
        count += (d + 1) * (d + 2) // 2
        degree = degree + jnp.where(index >= count, 1, 0)
    sign = jnp.where(degree % 2 == 0, 1.0, -1.0)
    return jnp.where(index < count, sign, 0.0)


def lane_signs():
    return signs_of(lax.broadcasted_iota(jnp.int32, (1, WIDE), 1))


def own_tables(own):
    own = own.astype(F32)
    own = jnp.concatenate([own, jnp.zeros((WIDE - own.shape[0], own.shape[1]), F32)], axis=0)
    signs = signs_of(lax.broadcasted_iota(jnp.int32, own.shape, 0))
    return own.astype(BF), (own * signs).astype(BF)


def dot_nt(a, b):
    return lax.dot_general(a, b, (((1,), (1,)), ((), ())), preferred_element_type=F32)


def dot_nn(a, b):
    return lax.dot_general(a, b, (((1,), (0,)), ((), ())), preferred_element_type=F32)


def split(x):
    high = x.astype(BF)
    low = (x - high.astype(F32)).astype(BF)
    return high, low


def one_hot(ids, size):
    rows = lax.broadcasted_iota(jnp.int32, (size, ids.shape[1]), 0)
    return jnp.where(rows == ids, 1.0, 0.0).astype(BF)


def pair_hots(pairs_ref, batch, count, first, second):
    targets = pairs_ref[0, batch, 0:1, :]
    sources = pairs_ref[0, batch, 1:2, :]
    spots = lax.broadcasted_iota(jnp.int32, targets.shape, 1)
    targets = jnp.where(spots < count, targets, -1)
    return one_hot(targets, first), one_hot(sources, second)


def scalar_row(read, count):
    lanes = lax.broadcasted_iota(jnp.int32, (1, LANES), 1)
    row = jnp.full((1, LANES), -1, jnp.int32)
    for i in range(count):
        row = jnp.where(lanes == i, read(i), row)
    return row


def pack_tiles(high, low, own):
    tail = high[:, LANES:] + pltpu.roll(low[:, LANES:], SHIFT, 1)
    tail = tail + pltpu.roll(own[:, LANES:], 2 * SHIFT, 1)
    return [high[:, :LANES], low[:, :LANES], own[:, :LANES], tail]


def unpack_tiles(tiles, coeffs):
    tail = tiles[3]
    lanes = lax.broadcasted_iota(jnp.int32, tail.shape, 1)
    parts = []
    for i in range(3):
        moved = tail if i == 0 else pltpu.roll(tail, LANES - i * SHIFT, 1)
        moved = jnp.where(lanes < coeffs - LANES, moved, 0.0)
        parts.append(jnp.concatenate([tiles[i], moved], axis=1).astype(BF))
    return parts


def gathered(batch_count, pairs_ref, first_batch, slots, flipped):
    counts = []
    for b in range(pairs_ref.shape[1]):
        hot_t, hot_u = pair_hots(
            pairs_ref, b, batch_count[0, first_batch + b], flipped.shape[1], slots
        )
        counts.append(dot_nt(hot_u, hot_t).astype(BF))
    return dot_nt(jnp.concatenate(counts, axis=0), flipped)


def back_terms(summed, mats, count_batches, first, slots):
    total = jnp.zeros((slots, PAD_ROWS), F32)
    for b in range(count_batches):
        high, low = split(summed[b * slots : (b + 1) * slots])
        both = dot_nt(jnp.concatenate([high, low], axis=0), mats[first + b])
        total = total + both[:slots] + both[slots:]
    total = total * lane_signs()[:, :PAD_ROWS]
    total = jnp.concatenate([total, jnp.zeros((slots, WIDE - PAD_ROWS), F32)], axis=1)
    high, low = split(total)
    return high.astype(F32), low.astype(F32)


def far_kernel(batch_count, own_ref, far_ref, far_send_ref, ops_ref, far_out, stage):
    cells = own_ref.shape[1]
    far_batches = far_ref.shape[1]
    far_slots = far_out.shape[0] // 4
    own_half, flipped = own_tables(own_ref[...])
    summed = gathered(
        batch_count, far_ref, batch_count.shape[1] - far_batches, far_slots, flipped
    )
    far_own = jnp.transpose(dot_nn(own_half, one_hot(far_send_ref[...], cells)))
    tiles = pack_tiles(*back_terms(summed, ops_ref, far_batches, 0, far_slots), far_own)
    for i in range(4):
        stage[pl.ds(i, far_slots, stride=4), :] = tiles[i]
    far_out[...] = stage[...].astype(BF)


def prepare_kernel(
    me, class_hbm, count_hbm, send_hbm, own_hbm, ops_hbm, group_hbm, group_out, near_ops, far_ops,
    batch_class, batch_count, group_send, own_ref, group_ref, ops_buf, low_table, high_table,
    near_mats, far_mats, small_sems, in_sems, out_sems,
):
    batches = batch_class.shape[1]
    coeffs, cells = own_ref.shape
    first_far = near_mats.shape[0]
    group_batches = group_ref.shape[1]
    first_group = first_far - group_batches
    group_slots = group_out.shape[0]
    small = [
        pltpu.make_async_copy(source, target, small_sems.at[i])
        for i, (source, target) in enumerate(
            (
                (class_hbm, batch_class),
                (count_hbm, batch_count),
                (send_hbm, group_send),
                (own_hbm, own_ref),
                (group_hbm, group_ref),
            )
        )
    ]
    for copy in small:
        copy.start()
    starts = [at for at in CHUNKS if at < coeffs] + [coeffs]
    chunks = [(at, end - at) for at, end in zip(starts, starts[1:])]
    copies = [
        pltpu.make_async_copy(
            ops_hbm.at[pl.ds(at, size)], ops_buf.at[pl.ds(at, size)], in_sems.at[i]
        )
        for i, (at, size) in enumerate(chunks)
    ]
    for copy in copies:
        copy.start()

    high_table[...] = jnp.zeros(high_table.shape, F32)
    low_table[coeffs * PITCH :, :] = jnp.zeros(((PAD_ROWS - coeffs) * PITCH, LANES), F32)
    for copy in small:
        copy.wait()

    rows = lax.broadcasted_iota(jnp.int32, (2 * batches, WIDE), 0)
    lanes = lax.broadcasted_iota(jnp.int32, (2 * batches, WIDE), 1)
    wanted = jnp.zeros((2 * batches, WIDE), jnp.int32)
    for i in range(batches):
        wanted = jnp.where(rows == i, batch_class[0, i], wanted)
        wanted = jnp.where(rows == batches + i, batch_class[0, i] + LANES, wanted)
    hot = jnp.where(lanes == wanted, 1.0, 0.0).astype(BF)

    own_half, flipped = own_tables(own_ref[...])

    group_sum = gathered(batch_count, group_ref, first_group, group_slots, flipped)
    row = scalar_row(lambda i: group_send[0, me[0], i // 8, i % 8], group_slots)
    group_own = jnp.transpose(dot_nn(own_half, one_hot(row, cells)))[:group_slots]

    def keep(at, picked):
        low_table[pl.ds(at * PITCH, batches), :] = picked[:, :LANES]
        high_table[pl.ds(at * PITCH, batches), : coeffs - LANES] = picked[:, LANES:]

    outs = []

    def take_out(c):
        at = chunks[c][0]
        size = (chunks[c + 1][0] if c + 1 < len(chunks) else PAD_ROWS) - at
        for i in range(batches):
            low = low_table[pl.ds(at * PITCH + i, size, stride=PITCH), :]
            high = high_table[pl.ds(at * PITCH + i, size, stride=PITCH), :]
            mats, place = (near_mats, i) if i < first_far else (far_mats, i - first_far)
            mats[place, at : at + size, :] = jnp.concatenate([low, high], axis=1).astype(BF)

    def send_out(c):
        at = chunks[c][0]
        size = (chunks[c + 1][0] if c + 1 < len(chunks) else PAD_ROWS) - at
        for k, (mats, target) in enumerate(((near_mats, near_ops), (far_mats, far_ops))):
            out = pltpu.make_async_copy(
                mats.at[:, pl.ds(at, size), :],
                target.at[:, pl.ds(at, size), :],
                out_sems.at[2 * c + k],
            )
            out.start()
            outs.append(out)

    for c, (copy, (at, size)) in enumerate(zip(copies, chunks)):
        copy.wait()
        for i in range(at, at + size, 2):
            if i + 1 < at + size:
                both = dot_nt(hot, jnp.concatenate([ops_buf[i], ops_buf[i + 1]], axis=1))
                keep(i, both[:batches])
                keep(i + 1, both[batches:])
            else:
                keep(i, dot_nt(hot[:batches, :LANES], ops_buf[i]))
        if c > 0:
            take_out(c - 1)
            send_out(c - 1)
    take_out(len(chunks) - 1)

    group_pair = back_terms(group_sum, near_mats, group_batches, first_group, group_slots)
    send_out(len(chunks) - 1)
    tiles = pack_tiles(*group_pair, group_own)
    group_out[...] = jnp.concatenate(tiles, axis=1).astype(BF)
    for out in outs:
        out.wait()


def forward_terms(total, counts, arrived, matrix):
    cells = total.shape[0]
    summed = dot_nn(jnp.concatenate(counts, axis=0), arrived)
    for b in range(len(counts)):
        high, low = split(summed[b * cells : (b + 1) * cells])
        both = dot_nt(jnp.concatenate([high, low], axis=0), matrix(b))
        total = total + both[:cells] + both[cells:]
    return total


def near_kernel(
    me, batch_count, group_send, own_ref, near_ref, group_ref, far_ref, group_in, ops_hbm,
    out_ref, counts_ref, ops_ref, sems,
):
    coeffs, cells = own_ref.shape
    near = near_ref.shape[1]
    group_slots = group_in.shape[0]
    parts = sems.shape[0]
    size = ops_hbm.shape[0] // parts
    copies = [
        pltpu.make_async_copy(
            ops_hbm.at[pl.ds(i * size, size)], ops_ref.at[pl.ds(i * size, size)], sems.at[i]
        )
        for i in range(parts)
    ]
    for copy in copies:
        copy.start()
    own_half, flipped = own_tables(own_ref[...])
    forward, backward, remote = [], [], []
    for b in range(near):
        hot_t, hot_u = pair_hots(near_ref, b, batch_count[0, b], cells, cells)
        forward.append(dot_nt(hot_t, hot_u).astype(BF))
        backward.append(dot_nt(hot_u, hot_t).astype(BF))
    ahead = dot_nt(jnp.concatenate(forward, axis=0), own_half)
    behind = dot_nt(jnp.concatenate(backward, axis=0), flipped)
    done = near
    for b in range(group_ref.shape[1]):
        hot_t, hot_u = pair_hots(group_ref, b, batch_count[0, done], cells, group_slots)
        remote.append(dot_nt(hot_t, hot_u).astype(BF))
        done += 1
    for b in range(far_ref.shape[1]):
        hot_t, hot_u = pair_hots(far_ref, b, batch_count[0, done], cells, LANES)
        counts_ref[b] = dot_nt(hot_t, hot_u).astype(BF)
        done += 1
    total = jnp.zeros((cells, PAD_ROWS), F32)
    mirrored = jnp.zeros((cells, PAD_ROWS), F32)
    for b in range(near):
        if b % size == 0:
            copies[b // size].wait()
        part = slice(b * cells, (b + 1) * cells)
        both = dot_nt(
            jnp.concatenate([*split(ahead[part]), *split(behind[part])], axis=0), ops_ref[b]
        )
        total = total + both[:cells] + both[cells : 2 * cells]
        mirrored = mirrored + both[2 * cells : 3 * cells] + both[3 * cells :]
    total = total + mirrored * lane_signs()[:, :PAD_ROWS]
    for copy in copies[-(-near // size) :]:
        copy.wait()
    tiles = [group_in[:, i * LANES : (i + 1) * LANES].astype(F32) for i in range(4)]
    high, low, arrived = unpack_tiles(tiles, coeffs)
    total = forward_terms(total, remote, arrived, lambda b: ops_ref[near + b])
    row = scalar_row(lambda i: group_send[0, me[0], i // 8, i % 8], group_slots)
    hot = one_hot(row, cells)[:, :group_slots]
    out_ref[...] = total + (dot_nn(hot, high) + dot_nn(hot, low))[:, :PAD_ROWS]


def finish_kernel(near_sum, counts_ref, ops_ref, far_send_ref, far_in, out_ref, stage):
    coeffs, cells = out_ref.shape
    far_slots = far_in.shape[0] // 4
    stage[...] = far_in[...].astype(F32)
    tiles = [stage[pl.ds(i, far_slots, stride=4), :] for i in range(4)]
    high, low, arrived = unpack_tiles(tiles, coeffs)
    counts = [counts_ref[b] for b in range(counts_ref.shape[0])]
    total = forward_terms(near_sum[...], counts, arrived, lambda b: ops_ref[b])
    hot = one_hot(far_send_ref[...], cells)
    total = total + (dot_nn(hot, high) + dot_nn(hot, low))[:, :PAD_ROWS]
    total = jnp.concatenate([total, jnp.zeros((cells, WIDE - PAD_ROWS), F32)], axis=1)
    out_ref[...] = jnp.transpose(total)[:coeffs]


def body(
    multipoles, operators, local_pairs, group_pairs, far_pairs, batch_class, batch_count,
    group_send, far_send,
):
    coeffs, cells = multipoles.shape
    batches = batch_class.shape[1]
    far_batches = far_pairs.shape[1]
    first_far = batches - far_batches
    group_size = lax.axis_size("grp")
    ranges = lax.axis_size("cells")
    far_slots = far_send.shape[1] * far_send.shape[2]
    far_send = far_send.reshape(1, far_slots)
    group_slots = group_size * group_send.shape[3]
    me = lax.axis_index("grp").reshape(1)
    smem = pl.BlockSpec(memory_space=pltpu.SMEM)
    vmem = pl.BlockSpec(memory_space=pltpu.VMEM)
    hbm = pl.BlockSpec(memory_space=pl.ANY)
    chunk_count = len(CHUNKS)
    group_rows, ops_near, ops_far = pl.pallas_call(
        prepare_kernel,
        in_specs=[smem] + [hbm] * 6,
        out_specs=[vmem, hbm, hbm],
        out_shape=[
            jax.ShapeDtypeStruct((group_slots, 4 * LANES), BF),
            jax.ShapeDtypeStruct((first_far, PAD_ROWS, WIDE), BF),
            jax.ShapeDtypeStruct((far_batches, PAD_ROWS, WIDE), BF),
        ],
        scratch_shapes=[
            pltpu.SMEM(batch_class.shape, jnp.int32),
            pltpu.SMEM(batch_count.shape, jnp.int32),
            pltpu.SMEM(group_send.shape, jnp.int32),
            pltpu.VMEM(multipoles.shape, BF),
            pltpu.VMEM(group_pairs.shape, jnp.int32),
            pltpu.VMEM(operators.shape, BF),
            pltpu.VMEM((PAD_ROWS * PITCH, LANES), F32),
            pltpu.VMEM((PAD_ROWS * PITCH, LANES), F32),
            pltpu.VMEM((first_far, PAD_ROWS, WIDE), BF),
            pltpu.VMEM((far_batches, PAD_ROWS, WIDE), BF),
            pltpu.SemaphoreType.DMA((5,)),
            pltpu.SemaphoreType.DMA((chunk_count,)),
            pltpu.SemaphoreType.DMA((2 * chunk_count,)),
        ],
        compiler_params=pltpu.CompilerParams(vmem_limit_bytes=60 * MIB),
        name="prepare",
    )(
        me, batch_class, batch_count, group_send, multipoles, operators, group_pairs,
    )
    far_rows = pl.pallas_call(
        far_kernel,
        in_specs=[smem] + [vmem] * 4,
        out_specs=vmem,
        out_shape=jax.ShapeDtypeStruct((far_slots * 4, LANES), BF),
        scratch_shapes=[pltpu.VMEM((far_slots * 4, LANES), F32)],
        compiler_params=pltpu.CompilerParams(vmem_limit_bytes=60 * MIB),
        cost_estimate=pl.CostEstimate(
            flops=10_000_000_000, bytes_accessed=20_000_000, transcendentals=0
        ),
        name="far",
    )(batch_count, multipoles, far_pairs, far_send, ops_far)
    group_got = lax.all_to_all(
        group_rows.reshape(group_size, -1, 4 * LANES), "grp", split_axis=0, concat_axis=0, tiled=True
    ).reshape(group_rows.shape)
    far_got = lax.all_to_all(
        far_rows.reshape(ranges, -1, LANES), "cells", split_axis=0, concat_axis=0, tiled=True
    ).reshape(far_rows.shape)
    near_sum, counts = pl.pallas_call(
        near_kernel,
        in_specs=[smem] * 3 + [vmem] * 5 + [hbm],
        out_specs=[vmem, vmem],
        out_shape=[
            jax.ShapeDtypeStruct((cells, PAD_ROWS), F32),
            jax.ShapeDtypeStruct((far_batches, cells, LANES), BF),
        ],
        scratch_shapes=[
            pltpu.VMEM((first_far, PAD_ROWS, WIDE), BF),
            pltpu.SemaphoreType.DMA((3,)),
        ],
        compiler_params=pltpu.CompilerParams(vmem_limit_bytes=NEAR_LIMIT),
        cost_estimate=pl.CostEstimate(
            flops=20_000_000_000, bytes_accessed=40_000_000, transcendentals=0
        ),
        name="near",
    )(
        me, batch_count, group_send, multipoles, local_pairs, group_pairs, far_pairs, group_got,
        ops_near,
    )
    return pl.pallas_call(
        finish_kernel,
        in_specs=[vmem] * 5,
        out_specs=vmem,
        out_shape=jax.ShapeDtypeStruct((coeffs, cells), F32),
        scratch_shapes=[pltpu.VMEM((far_slots * 4, LANES), F32)],
        compiler_params=pltpu.CompilerParams(vmem_limit_bytes=24 * MIB),
        name="finish",
    )(near_sum, counts, ops_far, far_send, far_got)


def solution(mesh):
    placed = (
        P(None, ("cells", "grp")),
        P(),
        P(("cells", "grp"), None, None, None),
        P(("cells", "grp"), None, None, None),
        P(("cells", "grp"), None, None, None),
        P(("cells", "grp"), None),
        P(("cells", "grp"), None),
        P("cells", None, None, None),
        P(("cells", "grp"), None, None),
    )
    return jax.shard_map(
        body, mesh=mesh, in_specs=placed, out_specs=P(None, ("cells", "grp")), check_vma=False
    )
```
